512 devices in a mesh: seq: 32 (over z, x), mem: 16 (over y, core).
Axes of the slice: x: 4, y: 8, z: 8, core: 2. Of those that a mesh axis runs over, the one named last changes fastest.
Arguments:
- queries: bfloat16 [65536, 2048], P(('seq', 'mem')), may hold values from -6 to 6
- keys: bfloat16 [65536, 2048], P(('seq', 'mem')), may hold values from -0.52734375 to 0.52734375
- values: bfloat16 [65536, 2048], P(('seq', 'mem')), may hold values from -6 to 6
- gamma: bfloat16 [65536, 16], P(('seq', 'mem')), as said below
- rate: bfloat16 [16, 16], replicated, as said below
- route_ids: int32 [65536, 2], P(('seq', 'mem')), may hold values from 0 to 15, all different within a row; in each aligned block of 128 rows (0 to 127, 128 to 255, ...) at most 24 rows name the same one
- route_weights: float32 [65536, 2], P(('seq', 'mem')), may hold values from 0.2 to 1
- norm_gain: float32 [2048], replicated, may hold values from 0.25 to 1.75
Outputs:
- mixed_out: bfloat16 [65536, 2048], P(('seq', 'mem'))
The draws below stay inside these ranges and needn't reach their ends.
Inputs may be any that keep to these rules, and one draw needn't show every extreme that they name: `route_ids`: each token names two different memories. The tokens of one device name one memory at most 24 times; some memory is named exactly 24 times by some device's tokens. `gamma`: Positive; from 0.5 up to 24576. `rate`: Positive; from 0.04 * 16 / 65536 up to 0.06.
All inputs are finite; a program needn't handle non-finite values.
Results may differ from the reference program's by a relative error of at most 0.0052.
Values may be sent and summed in bfloat16 or wider, within the bound.
No kernel may reach another device: no remote copies, remote signals or barrier semaphores. Data moves between devices by JAX's collectives and lax.ppermute only.
A program may use at most 128 MiB of HBM per device.

```python
import math
import jax
import jax.numpy as jnp
import numpy as np
from jax import lax

TOK_DEV = 128
HEADS = 16
HD = 128
BLOCK = 128
MEMORY_COUNT = 16
C = 24
SEQUENCE_TOKENS = 65536
SLOTS = 12288
N_SEQ = 32
N_MEM = 16


def draw_gamma(key, part):
    key_base = jax.random.fold_in(key, 11)
    key_position = jax.random.fold_in(key, 12)
    key_size = jax.random.fold_in(key, 13)
    baseline_rows = jnp.exp(jax.random.uniform(key_base, (SEQUENCE_TOKENS, HEADS), jnp.float32, math.log(0.5), math.log(2.0)))
    spike_positions = jax.random.randint(key_position, (2 * MEMORY_COUNT,), 0, SEQUENCE_TOKENS)
    spike_mask = jnp.zeros((SEQUENCE_TOKENS,), jnp.float32).at[spike_positions].set(1.0)
    spike_magnitude = 4.4 * SEQUENCE_TOKENS / MEMORY_COUNT * jax.random.uniform(key_size, (SEQUENCE_TOKENS, 1), jnp.float32, 1.0, 1.2)
    return jnp.where(spike_mask[:, None] > 0.5, spike_magnitude, baseline_rows).astype(jnp.bfloat16)


def draw_rate(key, part):
    lowest = 0.05 * MEMORY_COUNT / SEQUENCE_TOKENS
    share = 0.5
    slow_pick = jax.random.uniform(jax.random.fold_in(key, 21), (MEMORY_COUNT, HEADS), jnp.float32) < share
    slow_rates = lowest * jnp.exp(jax.random.uniform(jax.random.fold_in(key, 22), (MEMORY_COUNT, HEADS), jnp.float32, 0.0, math.log(2.0)))
    fast_rates = jnp.exp(jax.random.uniform(jax.random.fold_in(key, 23), (MEMORY_COUNT, HEADS), jnp.float32, math.log(0.01), math.log(0.05)))
    return jnp.where(slow_pick, slow_rates, fast_rates).astype(jnp.bfloat16)


def steps_of(stream_key, shape, shards, low, largest):
    loudness = 1.0
    for axis_at, parts in shards:
        heights = jax.random.uniform(jax.random.fold_in(jax.random.fold_in(stream_key, 6), axis_at), (parts,), jnp.float32, low / len(shards), largest / len(shards))
        loudness = loudness * jnp.repeat(jnp.exp(heights), shape[axis_at] // parts).reshape((-1,) + (1,) * (len(shape) - 1 - axis_at))
    return loudness


def deal_out(own_key, own, number, rows, amount, top, bound, slope):
    sequence = jax.random.permutation(own_key, amount)
    packed, usual = load_shares(amount, rows * top, bound, slope, True), load_shares(amount, rows * top, bound, slope, False)
    places = jnp.arange(amount)

    def named(lengths, rotation):
        used = int((lengths > 0).sum())
        fixed = max(1, used // 4)
        moved = fixed + (places - fixed + rotation * (used - fixed)) % max(1, amount - fixed)
        return jnp.zeros((amount,), jnp.int32).at[sequence[jnp.where(places < fixed, places, moved)]].set(jnp.asarray(lengths, jnp.int32))

    lengths = jnp.where(number % 4 == 0, named(packed, number // 4), named(usual, number - number // 4 - 1))
    mixed = jax.random.permutation(jax.random.fold_in(own, 3), amount)
    giver, taker = mixed[0:amount // 2 * 2:2], mixed[1:amount // 2 * 2:2]
    room = jnp.minimum(lengths[giver] - 1, bound - lengths[taker]) // 2
    room = jnp.where((giver == sequence[0]) | (taker == sequence[0]) | (lengths[taker] == 0), 0, jnp.maximum(room, 0))
    moved = jax.random.randint(jax.random.fold_in(own, 4), (amount // 2,), 0, 1 << 20) % (room + 1)
    lengths = lengths.at[giver].add(-moved).at[taker].add(moved)
    items = jnp.searchsorted(jnp.cumsum(lengths), jnp.arange(rows * top), side="right").astype(jnp.int32)
    table = items.reshape(top, rows).T
    table = table[jax.random.permutation(jax.random.fold_in(own, 1), rows)]
    rotation = jax.random.randint(jax.random.fold_in(own, 2), (rows, 1), 0, top)
    return jnp.take_along_axis(table, (jnp.arange(top)[None, :] + rotation) % top, axis=1)


def load_shares(amount, total, limit, skew, full):
    portions = [(1 << 20) // math.isqrt(rank ** skew) + 1 for rank in range(1, amount + 1)]
    largest = limit if full else min(limit, max(-(-total // amount), total * portions[0] // sum(portions)))
    least = 1 if total - largest >= amount - 1 else 0
    given, rest = [largest] + [least] * (amount - 1), total - largest - least * (amount - 1)
    while rest > 0:
        movable = [i for i in range(1, amount) if given[i] < largest] or [i for i in range(1, amount) if given[i] < limit]
        mass, budget = sum([portions[i] for i in movable]), rest
        for i in movable:
            addition = min(limit - given[i], max(1, budget * portions[i] // mass), rest)
            given[i] = given[i] + addition
            rest = rest - addition
    return np.array(given)


def centred(stream_key, dims, scale, most, split=(), kind=jnp.bfloat16):
    values = scale * jax.random.normal(stream_key, dims, jnp.float32)
    if split:
        values = values * steps_of(stream_key, dims, split, -0.22, 0.18)
    return jnp.clip(values, -most, most).astype(kind)


def setup_inputs(seed: int = 0) -> dict:
    key_list = jax.random.split(jax.random.key(seed), 9)
    queries = centred(key_list[0], (SEQUENCE_TOKENS, HEADS * HD), 1.0, 6.0, ((0, 512),))
    keys = centred(key_list[1], (SEQUENCE_TOKENS, HEADS * HD), 0.088, 0.52734375, ((0, 512),))
    values = centred(key_list[2], (SEQUENCE_TOKENS, HEADS * HD), 1.0, 6.0, ((0, 512),))
    gamma = draw_gamma(jax.random.fold_in(key_list[8], 71), 0)
    rate = draw_rate(jax.random.fold_in(key_list[8], 71), 0)
    route_ids_keys = jax.random.split(jax.random.fold_in(key_list[5], 1), SEQUENCE_TOKENS // TOK_DEV)
    route_ids_turns = jax.random.permutation(jax.random.fold_in(key_list[5], 3), SEQUENCE_TOKENS // TOK_DEV)
    route_ids = jax.vmap(lambda own, number: deal_out(jax.random.fold_in(key_list[5], 2), own, number, TOK_DEV, MEMORY_COUNT, 2, C, 2))(route_ids_keys, route_ids_turns).reshape((SEQUENCE_TOKENS, 2))
    route_weights = jnp.clip(0.2 + 0.8 * jax.random.uniform(key_list[6], (SEQUENCE_TOKENS, 2), jnp.float32) ** steps_of(key_list[6], (SEQUENCE_TOKENS, 2), ((0, 512),), -0.2, 0.2), 0.2, 1.0)
    norm_gain = jnp.clip(1.0 + 0.15 * jax.random.normal(key_list[7], (HEADS * HD,), jnp.float32), 0.25, 1.75)
    return dict(queries=queries, keys=keys, values=values, gamma=gamma, rate=rate, route_ids=route_ids, route_weights=route_weights, norm_gain=norm_gain)


epsilon = 1e-06

def reference(queries, keys, values, gamma, rate, route_ids, route_weights, norm_gain):
    feat_count = HEADS * HD
    block_count = SLOTS // BLOCK
    device_ids = (jnp.arange(SEQUENCE_TOKENS, dtype=jnp.int32) // TOK_DEV).astype(jnp.int32)
    causal = (jnp.arange(BLOCK)[:, None] >= jnp.arange(BLOCK)[None, :])[:, :, None]
    highest = lax.Precision.HIGHEST

    def memory_pass(totals, memory):
        route_hits = (route_ids == memory).astype(jnp.int32)
        route_rank = (jnp.cumsum(route_hits.reshape(N_SEQ * N_MEM, TOK_DEV * 2), axis=1).astype(jnp.int32).reshape(SEQUENCE_TOKENS, 2) - 1).astype(jnp.int32)
        token_rank = lax.optimization_barrier(jnp.sum(route_hits * route_rank, axis=1)).astype(jnp.int32)
        routed = lax.optimization_barrier(jnp.sum(route_hits, axis=1))
        slot_ids = jnp.where(routed > 0, device_ids * C + token_rank, SLOTS).astype(jnp.int32)
        query_slots = jnp.zeros((SLOTS, feat_count), jnp.bfloat16).at[slot_ids].set(queries, mode='drop')
        key_slots = jnp.zeros((SLOTS, feat_count), jnp.bfloat16).at[slot_ids].set(keys, mode='drop')
        value_slots = jnp.zeros((SLOTS, feat_count), jnp.bfloat16).at[slot_ids].set(values, mode='drop')
        gamma_slots = jnp.zeros((SLOTS, HEADS), jnp.bfloat16).at[slot_ids].set(gamma, mode='drop')
        rate_now = rate[memory].astype(jnp.float32)

        def block_step(state_now, inputs_now):
            query_rows, key_rows, value_rows, gamma_rows = inputs_now
            query32 = query_rows.astype(jnp.float32)
            key32 = key_rows.astype(jnp.float32)
            value32 = value_rows.astype(jnp.float32)
            levels = jnp.cumsum(-rate_now[None, :] * gamma_rows.astype(jnp.float32), axis=0)
            spread_log = levels[:, None, :] - levels[None, :, :]
            decays = jnp.exp(jnp.where(causal, spread_log, -1e+30))
            scores = jnp.einsum('thd,shd->tsh', query32, key32, precision=highest)
            weights = lax.optimization_barrier((decays * scores).astype(jnp.bfloat16)).astype(jnp.float32)
            intra_out = jnp.einsum('tsh,she->the', weights, value32, precision=highest)
            inter_out = jnp.einsum('thd,hde->the', query32 * jnp.exp(levels)[:, :, None], state_now, precision=highest)
            raw_out = intra_out + inter_out
            normed = raw_out * lax.rsqrt(lax.optimization_barrier(jnp.mean(raw_out * raw_out, axis=-1, keepdims=True)) + epsilon)
            last_level = levels[-1]
            keyed_rows = lax.optimization_barrier((key32 * jnp.exp(last_level[None, :] - levels)[:, :, None]).astype(jnp.bfloat16)).astype(jnp.float32)
            state_next = jnp.exp(last_level)[:, None, None] * state_now + jnp.einsum('shd,she->hde', keyed_rows, value32, precision=highest)
            return (state_next, normed.astype(jnp.bfloat16))
        start_state = jnp.zeros((HEADS, HD, HD), jnp.float32)
        block_inputs = (query_slots.reshape(block_count, BLOCK, HEADS, HD), key_slots.reshape(block_count, BLOCK, HEADS, HD), value_slots.reshape(block_count, BLOCK, HEADS, HD), gamma_slots.reshape(block_count, BLOCK, HEADS))
        _, block_outs = lax.scan(block_step, start_state, block_inputs)
        block_outs = block_outs.reshape(SLOTS, feat_count)
        picked = jnp.take(block_outs, jnp.minimum(slot_ids, SLOTS - 1), axis=0).astype(jnp.float32)
        weight = lax.optimization_barrier(jnp.sum(jnp.where(route_hits > 0, route_weights, jnp.float32(0.0)), axis=1))
        return (totals + weight[:, None] * picked, None)
    totals, _ = lax.scan(memory_pass, jnp.zeros((SEQUENCE_TOKENS, feat_count), jnp.float32), jnp.arange(N_MEM, dtype=jnp.int32))
    return (totals * norm_gain[None, :]).astype(jnp.bfloat16)
```

```python
import jax
import jax.numpy as jnp
from jax import lax
from jax.experimental import pallas as pl
from jax.experimental.pallas import tpu as pltpu
from jax.sharding import PartitionSpec as P

F32, BF16 = jnp.float32, jnp.bfloat16
TOK = 128
HD = 128
AUX = 16
PART_ROWS = 64
EPS = 1e-6
VMEM_LIMIT = 40 * 2**20


def iota(shape, dim):
    return lax.broadcasted_iota(jnp.int32, shape, dim)


def nt(a, b):
    return lax.dot_general(a, b, (((1,), (1,)), ((), ())), preferred_element_type=F32)


def tn(a, b):
    return lax.dot_general(a, b, (((0,), (0,)), ((), ())), preferred_element_type=F32)


def dot(a, b):
    return jnp.dot(a, b, preferred_element_type=F32)


def three_parts(x):
    hi = x.astype(BF16).astype(F32)
    mid = (x - hi).astype(BF16).astype(F32)
    return hi, mid, x - hi - mid


def pack_kernel(heads, q_ref, k_ref, v_ref, gamma_ref, ids_ref, weights_ref, out_ref):
    eye = (iota((TOK, TOK), 0) == iota((TOK, TOK), 1)).astype(BF16)
    gamma_rows = tn(gamma_ref[...], eye)
    ids = tn(ids_ref[...].astype(F32).astype(BF16), eye).astype(jnp.int32)
    w_hi, w_mid, w_lo = [tn(x.astype(BF16), eye) for x in three_parts(weights_ref[...])]
    memory = iota((heads, TOK), 0)
    hit0, hit1 = memory == ids[0:1], memory == ids[1:2]
    hits = jnp.where(hit0 | hit1, 1.0, 0.0).astype(BF16)
    earlier = (iota((TOK, TOK), 0) < iota((TOK, TOK), 1)).astype(BF16)
    before = dot(hits, earlier)
    rank0 = jnp.sum(jnp.where(hit0, before, 0.0), axis=0, keepdims=True)
    rank1 = jnp.sum(jnp.where(hit1, before, 0.0), axis=0, keepdims=True)
    row = iota((AUX, TOK), 0)
    shared = jnp.zeros((AUX, TOK), F32)
    entries = [ids[0:1].astype(F32), rank0, ids[1:2].astype(F32), rank1]
    for part in (w_hi, w_mid, w_lo):
        entries += [part[0:1], part[1:2]]
    for at, entry in enumerate(entries):
        shared = jnp.where(row == at + 1, entry, shared)
    for h in range(heads):
        lanes = slice(h * HD, (h + 1) * HD)
        out_ref[h, 0:TOK] = k_ref[:, lanes]
        out_ref[h, TOK : 2 * TOK] = v_ref[:, lanes]
        out_ref[h, 2 * TOK : 3 * TOK] = q_ref[:, lanes]
        aux = jnp.where(row == 0, gamma_rows[h : h + 1], shared)
        out_ref[h, 3 * TOK : 3 * TOK + AUX] = aux.astype(BF16)


def head_rates(rate_ref, head, scratch_ref):
    rates = rate_ref[...].astype(F32)
    mine = jnp.where(iota(rates.shape, 1) == head, rates, 0.0)
    scratch_ref[...] = jnp.broadcast_to(jnp.sum(mine, axis=1, keepdims=True), scratch_ref.shape)


def gather_kernel(memories, cap, in_ref, rate_ref, slots_ref, update_ref, rates_ref, after_ref):
    sources = in_ref.shape[0]
    slots = sources * cap
    head_rates(rate_ref, lax.axis_index("mem"), rates_ref)
    after_ref[...] = (iota((slots, slots), 1) > iota((slots, slots), 0)).astype(BF16)
    place = iota((memories * 2 * cap, TOK), 0)
    same = iota((TOK, TOK), 0) == iota((TOK, TOK), 1)
    ones = jnp.ones((TOK, HD), BF16)

    def gather(pair, carry):
        select, rows = [], []
        for side in range(2):
            source = 2 * pair + side
            aux = in_ref[source, 3 * TOK : 3 * TOK + AUX].astype(F32)
            at = aux[0:8].astype(jnp.int32)
            first = at[1:2] * (2 * cap) + at[2:3] + side * cap
            second = at[3:4] * (2 * cap) + at[4:5] + side * cap
            hit = (place == first) | (place == second)
            select.append(jnp.where(hit, 1.0, 0.0).astype(BF16))
            gamma = dot(jnp.where(same, aux[0:1], 0.0).astype(BF16), ones).astype(BF16)
            k = in_ref[source, 0:TOK]
            v = in_ref[source, TOK : 2 * TOK]
            q = in_ref[source, 2 * TOK : 3 * TOK]
            rows.append(jnp.concatenate([k, v, q, gamma], axis=1))
        got = dot(jnp.concatenate(select, axis=1), jnp.concatenate(rows, axis=0)).astype(BF16)
        at = pl.ds(pl.multiple_of(pair * 2 * cap, 2 * cap), 2 * cap)
        for m in range(memories):
            slots_ref[m, at, :] = got[m * 2 * cap : (m + 1) * 2 * cap]
        return carry

    lax.fori_loop(0, sources // 2, gather, 0)

    def update(m, carry):
        k = slots_ref[m, :, 0:HD].astype(F32)
        v = slots_ref[m, :, HD : 2 * HD]
        gamma = slots_ref[m, :, 3 * HD : 4 * HD]
        rate = rates_ref[pl.ds(m, 1), :]
        rest = dot(after_ref[...], gamma)
        kd = (k * jnp.exp(-rate * rest)).astype(BF16)
        added = tn(kd, v).astype(BF16)
        total = -rate * jnp.sum(gamma.astype(F32), axis=0, keepdims=True)
        row = iota((AUX, HD), 0)
        aux = jnp.zeros((AUX, HD), F32)
        for at, part in enumerate(three_parts(total)):
            aux = jnp.where(row == at, part, aux)
        for half in range(2):
            update_ref[2 * m + half, 0:PART_ROWS] = added[half * PART_ROWS : (half + 1) * PART_ROWS]
            update_ref[2 * m + half, PART_ROWS : PART_ROWS + AUX] = aux.astype(BF16)
        return carry

    lax.fori_loop(0, memories, update, 0)


def scan_kernel(in_ref, out_ref):
    state = jnp.zeros((PART_ROWS, HD), F32)
    for part in range(in_ref.shape[0]):
        out_ref[part] = state.astype(BF16)
        aux = in_ref[part, PART_ROWS : PART_ROWS + AUX].astype(F32)
        fade = jnp.exp(aux[0:1] + aux[1:2] + aux[2:3])
        state = fade * state + in_ref[part, 0:PART_ROWS].astype(F32)


def intra_kernel(slots_ref, rate_ref, raw_ref, fade_ref, rates_ref, upto_ref):
    memories, slots, _ = slots_ref.shape
    head_rates(rate_ref, lax.axis_index("mem"), rates_ref)
    causal = iota((slots, slots), 0) >= iota((slots, slots), 1)
    upto_ref[...] = causal.astype(BF16)

    def one(m, carry):
        k = slots_ref[m, :, 0:HD]
        v = slots_ref[m, :, HD : 2 * HD]
        q = slots_ref[m, :, 2 * HD : 3 * HD]
        gamma = slots_ref[m, :, 3 * HD : 4 * HD]
        rate = rates_ref[pl.ds(m, 1), :]
        wide = jnp.concatenate([gamma] * (slots // HD), axis=1).astype(F32)
        later = iota((slots, slots), 0) > iota((slots, slots), 1)
        spread = dot(upto_ref[...], jnp.where(later, wide, 0.0).astype(BF16))
        fade_ref[m] = jnp.exp(-rate * dot(upto_ref[...], gamma))
        wide_rate = jnp.concatenate([rate] * (slots // HD), axis=1)
        decay = jnp.exp(-wide_rate * spread)
        keep = iota((slots, slots), 0) >= iota((slots, slots), 1)
        weights = jnp.where(keep, decay * nt(q, k), 0.0).astype(BF16)
        raw_ref[m] = dot(weights, v)
        return carry

    lax.fori_loop(0, memories, one, 0)


def finish_kernel(cap, in_ref, slots_ref, raw_ref, fade_ref, state_ref, gain_ref, out_ref, made_ref):
    memories, slots, _ = slots_ref.shape
    sources = in_ref.shape[0]

    def one(m, carry):
        q = slots_ref[m, :, 2 * HD : 3 * HD]
        raw = raw_ref[m] + fade_ref[m] * dot(q, state_ref[m])
        mean = jnp.mean(raw * raw, axis=1, keepdims=True)
        made_ref[m] = (raw * lax.rsqrt(mean + EPS)).astype(BF16)
        return carry

    lax.fori_loop(0, memories, one, 0)
    gain = gain_ref[pl.ds(lax.axis_index("mem"), 1), :]
    width = memories * 2 * cap
    place = iota((TOK, width), 1)
    eye = (iota((TOK, TOK), 0) == iota((TOK, TOK), 1)).astype(BF16)

    def mix(pair, carry):
        at = pl.ds(pl.multiple_of(pair * 2 * cap, 2 * cap), 2 * cap)
        rows = jnp.concatenate([made_ref[m, at, :] for m in range(memories)], axis=0)
        for side in range(2):
            source = 2 * pair + side
            aux = nt(eye, in_ref[source, 3 * TOK : 3 * TOK + AUX])
            number = aux.astype(jnp.int32)
            first = number[:, 1:2] * (2 * cap) + number[:, 2:3] + side * cap
            second = number[:, 3:4] * (2 * cap) + number[:, 4:5] + side * cap
            w0 = aux[:, 5:6] + aux[:, 7:8] + aux[:, 9:10]
            w1 = aux[:, 6:7] + aux[:, 8:9] + aux[:, 10:11]
            pick0 = jnp.where(place == first, 1.0, 0.0).astype(BF16)
            pick1 = jnp.where(place == second, 1.0, 0.0).astype(BF16)
            mixed = w0 * dot(pick0, rows) + w1 * dot(pick1, rows)
            out_ref[source] = (gain * mixed).astype(BF16)
        return carry

    lax.fori_loop(0, sources // 2, mix, 0)


def unpack_kernel(in_ref, out_ref):
    for h in range(in_ref.shape[0]):
        out_ref[:, h * HD : (h + 1) * HD] = in_ref[h]


def call(kernel, outs, scratch=(), flops=0, moved=0, exps=0):
    return pl.pallas_call(
        kernel,
        out_shape=outs,
        scratch_shapes=list(scratch),
        compiler_params=pltpu.CompilerParams(vmem_limit_bytes=VMEM_LIMIT),
        cost_estimate=pl.CostEstimate(flops=flops, bytes_accessed=moved, transcendentals=exps),
    )


def body(queries, keys, values, gamma, rate, route_ids, route_weights, norm_gain):
    heads = gamma.shape[1]
    memories = rate.shape[0]
    sources = lax.axis_size("mem")
    parts = lax.axis_size("seq")
    cap = 3 * TOK // memories
    slots = sources * cap
    like = jax.ShapeDtypeStruct

    send = call(
        lambda *refs: pack_kernel(heads, *refs),
        like((heads, 3 * TOK + AUX, HD), BF16),
    )(queries, keys, values, gamma, route_ids, route_weights)
    arrived = lax.all_to_all(send, "mem", 0, 0, tiled=True)

    rates = pltpu.VMEM((memories, HD), F32)
    square = pltpu.VMEM((slots, slots), BF16)
    slot_rows, update = call(
        lambda *refs: gather_kernel(memories, cap, *refs),
        (
            like((memories, slots, 4 * HD), BF16),
            like((parts, PART_ROWS + AUX, HD), BF16),
        ),
        (rates, square),
    )(arrived, rate)
    pieces = lax.all_to_all(update, "seq", 0, 0, tiled=True)
    raw, fade = call(
        intra_kernel,
        (like((memories, slots, HD), F32), like((memories, slots, HD), F32)),
        (rates, square),
        flops=memories * slots * slots * HD * 10,
        moved=memories * slots * HD * 16,
        exps=memories * slots * slots,
    )(slot_rows, rate)
    before = call(scan_kernel, like((parts, PART_ROWS, HD), BF16))(pieces)
    state = lax.all_to_all(before, "seq", 0, 0, tiled=True).reshape(memories, HD, HD)
    mixed = call(
        lambda *refs: finish_kernel(cap, *refs),
        like((sources, TOK, HD), BF16),
        (pltpu.VMEM((memories, slots, HD), BF16),),
    )(arrived, slot_rows, raw, fade, state, norm_gain.reshape(heads, HD))
    returned = lax.all_to_all(mixed, "mem", 0, 0, tiled=True)
    return call(unpack_kernel, like((TOK, heads * HD), BF16))(returned)


def solution(mesh):
    split = P(("seq", "mem"), None)
    return jax.shard_map(
        body,
        mesh=mesh,
        in_specs=(split, split, split, split, P(), split, split, P()),
        out_specs=split,
        check_vma=False,
    )
```

```python
import jax
import jax.numpy as jnp
from jax import lax
from jax.experimental import pallas as pl
from jax.experimental.pallas import tpu as pltpu
from jax.sharding import PartitionSpec as P

F32, BF16 = jnp.float32, jnp.bfloat16
TOK = 128
HD = 128
AUX = 16
KV = 2 * TOK + AUX
PART_ROWS = 64
EPS = 1e-6
VMEM_ALL = 58_000_000


def iota(shape, dim):
    return lax.broadcasted_iota(jnp.int32, shape, dim)


def nt(a, b):
    return lax.dot_general(a, b, (((1,), (1,)), ((), ())), preferred_element_type=F32)


def tn(a, b):
    return lax.dot_general(a, b, (((0,), (0,)), ((), ())), preferred_element_type=F32)


def dot(a, b):
    return jnp.dot(a, b, preferred_element_type=F32)


def three_parts(x):
    hi = x.astype(BF16).astype(F32)
    mid = (x - hi).astype(BF16).astype(F32)
    return hi, mid, x - hi - mid


def own_head():
    return lax.axis_index("mem")


def pack_kernel(
    heads, q_ref, k_ref, v_ref, gamma_ref, ids_ref, weights_ref, out_ref, sem
):
    copies = []
    for h in range(heads):
        for at, ref in ((0, k_ref), (TOK, v_ref), (KV, q_ref)):
            copies.append(
                pltpu.make_async_copy(
                    ref.at[:, h * HD : (h + 1) * HD],
                    out_ref.at[h, at : at + TOK],
                    sem.at[len(copies)],
                )
            )
    for copy in copies:
        copy.start()
    ids = ids_ref[...]
    w_hi, w_mid, w_lo = three_parts(weights_ref[...])
    memory = iota((heads, TOK), 0)
    hit0, hit1 = memory == ids[0:1], memory == ids[1:2]
    hits = jnp.where(hit0 | hit1, 1.0, 0.0).astype(BF16)
    earlier = (iota((TOK, TOK), 0) < iota((TOK, TOK), 1)).astype(BF16)
    before = dot(hits, earlier)
    rank0 = jnp.sum(jnp.where(hit0, before, 0.0), axis=0, keepdims=True)
    rank1 = jnp.sum(jnp.where(hit1, before, 0.0), axis=0, keepdims=True)
    row = iota((AUX, TOK), 0)
    shared = jnp.zeros((AUX, TOK), F32)
    entries = [ids[0:1].astype(F32), rank0, ids[1:2].astype(F32), rank1]
    for part in (w_hi, w_mid, w_lo):
        entries += [part[0:1], part[1:2]]
    for at, entry in enumerate(entries):
        shared = jnp.where(row == at + 1, entry, shared)
    gamma_rows = gamma_ref[...].astype(F32)
    for h in range(heads):
        aux = jnp.where(row == 0, gamma_rows[h : h + 1], shared)
        out_ref[h, 2 * TOK : KV] = aux.astype(BF16)
    for copy in copies:
        copy.wait()


def head_rates(rate_ref, head, scratch_ref):
    rates = rate_ref[...].astype(F32)
    mine = jnp.where(iota(rates.shape, 1) == head, rates, 0.0)
    scratch_ref[...] = jnp.broadcast_to(jnp.sum(mine, axis=1, keepdims=True), scratch_ref.shape)


def slot_ids(aux, cap, side):
    at = aux[0:8].astype(jnp.int32)
    first = at[1:2] * (2 * cap) + at[2:3] + side * cap
    second = at[3:4] * (2 * cap) + at[4:5] + side * cap
    return first, second


def gather_kernel(
    cap, in_ref, rate_ref, slots_out, update_ref, rows_ref, slots_ref, rest_ref, rates_ref, later_ref, sem, slots_sem
):
    sources = in_ref.shape[0]
    memories, slots, _ = slots_ref.shape
    width = memories * 2 * cap

    def arriving(source):
        return pltpu.make_async_copy(in_ref.at[source, 0:KV], rows_ref.at[source], sem.at[source])

    for source in range(sources):
        arriving(source).start()
    head_rates(rate_ref, own_head(), rates_ref)
    after = (iota((TOK, TOK), 0) > iota((TOK, TOK), 1)).astype(BF16)
    memory = iota((memories, TOK), 0)
    for source in range(sources):
        arriving(source).wait()

    hits, gammas = [], []
    for source in range(sources):
        aux = rows_ref[source, 2 * TOK : KV].astype(F32)
        at = aux.astype(jnp.int32)
        hit = (memory == at[1:2]) | (memory == at[3:4])
        gammas.append(jnp.where(hit, aux[0:1], 0.0))
    inside = dot(jnp.concatenate(gammas, axis=0).astype(BF16), after)
    behind = jnp.zeros((memories, 1), F32)
    for source in reversed(range(sources)):
        own = inside[source * memories : (source + 1) * memories]
        later_ref[source] = own + behind
        behind = behind + own[:, 0:1] + gammas[source][:, 0:1]
    total = -rates_ref[...] * behind

    place = iota((width, TOK), 0)

    def gather(pair, carry):
        rows, select, rest = [], [], jnp.zeros((width, TOK), F32)
        for side in range(2):
            source = 2 * pair + side
            aux = rows_ref[source, 2 * TOK : KV].astype(F32)
            at = aux.astype(jnp.int32)
            later = later_ref[source]
            rest0 = jnp.sum(jnp.where(memory == at[1:2], later, 0.0), axis=0, keepdims=True)
            rest1 = jnp.sum(jnp.where(memory == at[3:4], later, 0.0), axis=0, keepdims=True)
            first, second = slot_ids(aux, cap, side)
            hit0, hit1 = place == first, place == second
            select.append(jnp.where(hit0 | hit1, 1.0, 0.0).astype(BF16))
            rest = rest + jnp.where(hit0, rest0, jnp.where(hit1, rest1, 0.0))
            rows.append(
                jnp.concatenate([rows_ref[source, 0:TOK], rows_ref[source, TOK : 2 * TOK]], axis=1)
            )
        rest = jnp.broadcast_to(jnp.sum(rest, axis=1, keepdims=True), (width, HD))
        got = dot(jnp.concatenate(select, axis=1), jnp.concatenate(rows, axis=0)).astype(BF16)
        at = pl.ds(pl.multiple_of(pair * 2 * cap, 2 * cap), 2 * cap)
        for m in range(memories):
            slots_ref[m, at, :] = got[m * 2 * cap : (m + 1) * 2 * cap]
            rest_ref[m, at, :] = rest[m * 2 * cap : (m + 1) * 2 * cap]
        leaving(pair).start()
        return carry

    def leaving(pair):
        at = pl.ds(pl.multiple_of(pair * 2 * cap, 2 * cap), 2 * cap)
        return pltpu.make_async_copy(slots_ref.at[:, at], slots_out.at[:, at], slots_sem.at[pair])

    lax.fori_loop(0, sources // 2, gather, 0)

    def update(m, carry):
        k = slots_ref[m, :, 0:HD].astype(F32)
        v = slots_ref[m, :, HD : 2 * HD]
        kd = (k * jnp.exp(-rates_ref[pl.ds(m, 1), :] * rest_ref[m])).astype(BF16)
        added = tn(kd, v).astype(BF16)
        for half in range(2):
            part = added[half * PART_ROWS : (half + 1) * PART_ROWS]
            update_ref[2 * m + half, 0:PART_ROWS] = part
        return carry

    lax.fori_loop(0, memories, update, 0, unroll=2)
    row = iota((AUX, HD), 0)
    for m in range(memories):
        aux = jnp.zeros((AUX, HD), F32)
        for at, part in enumerate(three_parts(total[m : m + 1])):
            aux = jnp.where(row == at, part, aux)
        for half in range(2):
            update_ref[2 * m + half, PART_ROWS : PART_ROWS + AUX] = aux.astype(BF16)
    for pair in range(sources // 2):
        leaving(pair).wait()


def scan_kernel(in_ref, out_ref):
    state = jnp.zeros((PART_ROWS, HD), F32)
    for part in range(in_ref.shape[0]):
        out_ref[part] = state.astype(BF16)
        aux = in_ref[part, PART_ROWS : PART_ROWS + AUX].astype(F32)
        fade = jnp.exp(aux[0:1] + aux[1:2] + aux[2:3])
        state = fade * state + in_ref[part, 0:PART_ROWS].astype(F32)


def route_kernel(cap, in_ref, slots_ref, pick_ref):
    memories = slots_ref.shape[0]
    width = memories * 2 * cap
    eye = iota((TOK, TOK), 0) == iota((TOK, TOK), 1)
    ones = jnp.ones((TOK, HD), BF16)
    place = iota((width, TOK), 0)
    rows, select = [], []
    for side in range(2):
        aux = in_ref[side, 2 * TOK : KV].astype(F32)
        gamma = dot(jnp.where(eye, aux[0:1], 0.0).astype(BF16), ones).astype(BF16)
        rows.append(jnp.concatenate([in_ref[side, KV : KV + TOK], gamma], axis=1))
        first, second = slot_ids(aux, cap, side)
        hit = (place == first) | (place == second)
        select.append(jnp.where(hit, 1.0, 0.0).astype(BF16))
    got = dot(jnp.concatenate(select, axis=1), jnp.concatenate(rows, axis=0)).astype(BF16)
    for m in range(memories):
        slots_ref[m] = got[m * 2 * cap : (m + 1) * 2 * cap]
    place = iota((TOK, width), 1)
    for side in range(2):
        aux = nt(eye.astype(BF16), in_ref[side, 2 * TOK : KV])
        at = aux.astype(jnp.int32)
        first = at[:, 1:2] * (2 * cap) + at[:, 2:3] + side * cap
        second = at[:, 3:4] * (2 * cap) + at[:, 4:5] + side * cap
        w0 = aux[:, 5:6] + aux[:, 7:8] + aux[:, 9:10]
        w1 = aux[:, 6:7] + aux[:, 8:9] + aux[:, 10:11]
        pick = jnp.where(place == first, w0, jnp.where(place == second, w1, 0.0))
        pick_ref[0, side * TOK : (side + 1) * TOK] = pick.astype(BF16)


def intra_kernel(kv_ref, qg_ref, rate_ref, raw_ref, faded_ref, rates_ref, sums_ref):
    slots = kv_ref.shape[1]
    m = pl.program_id(0)
    tri = iota((TOK, TOK), 0) - iota((TOK, TOK), 1)

    @pl.when(m == 0)
    def _():
        head_rates(rate_ref, own_head(), rates_ref)
        sums_ref[0:TOK] = (tri >= 0).astype(BF16)
        sums_ref[TOK : 2 * TOK] = (tri < 0).astype(BF16)

    rate = rates_ref[pl.ds(m, 1), :]
    behind = []
    faded_all = jnp.ones((1, HD), F32)
    for b in range(slots // TOK):
        at = slice(b * TOK, (b + 1) * TOK)
        q = qg_ref[0, at, 0:HD]
        gamma = qg_ref[0, at, HD : 2 * HD]
        masked = jnp.where(tri > 0, gamma.astype(F32), 0.0).astype(BF16)
        sums = dot(sums_ref[...], jnp.concatenate([masked, gamma], axis=1))
        inside = jnp.where(tri >= 0, jnp.exp(-rate * sums[0:TOK, 0:TOK]), 0.0)
        fade = jnp.exp(-rate * sums[0:TOK, TOK : 2 * TOK])
        faded_ref[0, at] = (q.astype(F32) * (fade * faded_all)).astype(BF16)
        decay = jnp.concatenate([fade * row for row in behind] + [inside], axis=1)
        scores = nt(q, kv_ref[0, 0 : (b + 1) * TOK, 0:HD])
        weights = (decay * scores).astype(BF16)
        raw_ref[0, at] = dot(weights, kv_ref[0, 0 : (b + 1) * TOK, HD : 2 * HD])
        whole = fade[TOK - 1 : TOK]
        faded_all = faded_all * whole
        rest = jnp.exp(-rate * sums[TOK : 2 * TOK, TOK : 2 * TOK])
        behind = [row * whole for row in behind] + [rest.T]


def finish_kernel(
    cap, faded_hbm, raw_hbm, pick_hbm, state_ref, gain_ref, out_ref, faded_ref, raw_ref, pick_ref, made_ref, sems, pick_sem
):
    memories = faded_ref.shape[0]
    pairs = pick_ref.shape[0]

    def arriving(m):
        return (
            pltpu.make_async_copy(faded_hbm.at[m], faded_ref.at[m], sems.at[0, m]),
            pltpu.make_async_copy(raw_hbm.at[m], raw_ref.at[m], sems.at[1, m]),
        )

    picks = pltpu.make_async_copy(pick_hbm, pick_ref, pick_sem)
    for m in range(memories):
        for copy in arriving(m):
            copy.start()
    picks.start()

    def one(m, carry):
        for copy in arriving(m):
            copy.wait()
        raw = raw_ref[m] + dot(faded_ref[m], state_ref[m])
        mean = jnp.mean(raw * raw, axis=1, keepdims=True)
        made_ref[m] = (raw * lax.rsqrt(mean + EPS)).astype(BF16)
        return carry

    lax.fori_loop(0, memories, one, 0, unroll=2)
    picks.wait()
    gain = gain_ref[pl.ds(own_head(), 1), :]

    def mix(pair, carry):
        at = pl.ds(pl.multiple_of(pair * 2 * cap, 2 * cap), 2 * cap)
        rows = jnp.concatenate([made_ref[m, at, :] for m in range(memories)], axis=0)
        mixed = (gain * dot(pick_ref[pair], rows)).astype(BF16)
        for side in range(2):
            out_ref[2 * pair + side] = mixed[side * TOK : (side + 1) * TOK]
        return carry

    lax.fori_loop(0, pairs, mix, 0, unroll=2)


def unpack_kernel(in_ref, out_ref):
    for h in range(in_ref.shape[0]):
        out_ref[:, h * HD : (h + 1) * HD] = in_ref[h]


like = jax.ShapeDtypeStruct
ANY = pl.BlockSpec(memory_space=pl.ANY)
WHOLE = pl.BlockSpec(memory_space=pltpu.VMEM)
DMA = pltpu.SemaphoreType.DMA


def call(kernel, outs, ins, out_specs, room, scratch=(), grid=(), flops=0, moved=0):
    return pl.pallas_call(
        kernel,
        out_shape=outs,
        grid=grid,
        in_specs=ins,
        out_specs=out_specs,
        scratch_shapes=list(scratch),
        compiler_params=pltpu.CompilerParams(vmem_limit_bytes=VMEM_ALL - room),
        cost_estimate=pl.CostEstimate(flops=flops, bytes_accessed=moved, transcendentals=0),
    )


def pack(heads):
    return call(
        lambda *refs: pack_kernel(heads, *refs),
        like((heads, KV + TOK, HD), BF16),
        [ANY, ANY, ANY, WHOLE, WHOLE, WHOLE],
        WHOLE,
        -2_000_000,
        (DMA((3 * heads,)),),
    )


def gather(memories, sources, parts):
    cap = 3 * TOK // memories
    slots = sources * cap
    return call(
        lambda *refs: gather_kernel(cap, *refs),
        (
            like((memories, slots, 2 * HD), BF16),
            like((parts, PART_ROWS + AUX, HD), BF16),
        ),
        [ANY, WHOLE],
        (ANY, WHOLE),
        2_500_000,
        (
            pltpu.VMEM((sources, KV, HD), BF16),
            pltpu.VMEM((memories, slots, 2 * HD), BF16),
            pltpu.VMEM((memories, slots, HD), F32),
            pltpu.VMEM((memories, HD), F32),
            pltpu.VMEM((sources, memories, TOK), F32),
            DMA((sources,)),
            DMA((sources // 2,)),
        ),
    )


def scan(parts):
    return call(scan_kernel, like((parts, PART_ROWS, HD), BF16), [WHOLE], WHOLE, 40_000_000)


def route(memories, sources):
    cap = 3 * TOK // memories
    slots = sources * cap
    pairs = sources // 2
    width = memories * 2 * cap
    return call(
        lambda *refs: route_kernel(cap, *refs),
        (like((memories, slots, 2 * HD), BF16), like((pairs, 2 * TOK, width), BF16)),
        [pl.BlockSpec((2, KV + TOK, HD), lambda p: (p, 0, 0))],
        (
            pl.BlockSpec((memories, 2 * cap, 2 * HD), lambda p: (0, p, 0)),
            pl.BlockSpec((1, 2 * TOK, width), lambda p: (p, 0, 0)),
        ),
        1_000_000,
        grid=(pairs,),
        flops=10**10,
        moved=8 * 2**20,
    )


def intra(memories, sources):
    slots = sources * (3 * TOK // memories)
    one = pl.BlockSpec((1, slots, HD), lambda m: (m, 0, 0))
    two = pl.BlockSpec((1, slots, 2 * HD), lambda m: (m, 0, 0))
    return call(
        intra_kernel,
        (like((memories, slots, HD), F32), like((memories, slots, HD), BF16)),
        [two, two, WHOLE],
        (one, one),
        1_000_000,
        (pltpu.VMEM((memories, HD), F32), pltpu.VMEM((2 * TOK, TOK), BF16)),
        grid=(memories,),
        flops=10**10,
        moved=10 * 2**20,
    )


def finish(memories, sources):
    cap = 3 * TOK // memories
    slots = sources * cap
    pairs = sources // 2
    return call(
        lambda *refs: finish_kernel(cap, *refs),
        like((sources, TOK, HD), BF16),
        [ANY, ANY, ANY, WHOLE, WHOLE],
        WHOLE,
        1_300_000,
        (
            pltpu.VMEM((memories, slots, HD), BF16),
            pltpu.VMEM((memories, slots, HD), F32),
            pltpu.VMEM((pairs, 2 * TOK, memories * 2 * cap), BF16),
            pltpu.VMEM((memories, slots, HD), BF16),
            DMA((2, memories)),
            DMA(()),
        ),
    )


def unpack(heads):
    return call(unpack_kernel, like((TOK, heads * HD), BF16), [WHOLE], WHOLE, 40_000_000)


def body(queries, keys, values, gamma, rate, route_ids, route_weights, norm_gain):
    heads = gamma.shape[1]
    memories = rate.shape[0]
    sources = lax.axis_size("mem")
    parts = lax.axis_size("seq")
    send = pack(heads)(queries, keys, values, gamma.T, route_ids.T, route_weights.T)
    arrived = lax.all_to_all(send, "mem", 0, 0, tiled=True)
    slot_rows, update = gather(memories, sources, parts)(arrived, rate)
    pieces = lax.all_to_all(update, "seq", 0, 0, tiled=True)
    q_rows, pick = route(memories, sources)(arrived)
    pieces, q_rows, pick = lax.optimization_barrier((pieces, q_rows, pick))
    before = scan(parts)(pieces)
    raw, faded = intra(memories, sources)(slot_rows, q_rows, rate)
    state = lax.all_to_all(before, "seq", 0, 0, tiled=True).reshape(memories, HD, HD)
    gain = norm_gain.reshape(heads, HD)
    mixed = finish(memories, sources)(faded, raw, pick, state, gain)
    returned = lax.all_to_all(mixed, "mem", 0, 0, tiled=True)
    return unpack(heads)(returned)


def solution(mesh):
    split = P(("seq", "mem"), None)
    return jax.shard_map(
        body,
        mesh=mesh,
        in_specs=(split, split, split, split, P(), split, split, P()),
        out_specs=split,
        check_vma=False,
    )
```

```python
import jax
import jax.numpy as jnp
from jax import lax
from jax.experimental import pallas as pl
from jax.experimental.pallas import tpu as pltpu
from jax.sharding import PartitionSpec as P

F32, BF16 = jnp.float32, jnp.bfloat16
TOK = 128
HD = 128
AUX = 16
QA = TOK + AUX
PART_ROWS = 64
EPS = 1e-6
VMEM_ALL = 58_000_000


def iota(shape, dim):
    return lax.broadcasted_iota(jnp.int32, shape, dim)


def nt(a, b):
    return lax.dot_general(a, b, (((1,), (1,)), ((), ())), preferred_element_type=F32)


def tn(a, b):
    return lax.dot_general(a, b, (((0,), (0,)), ((), ())), preferred_element_type=F32)


def dot(a, b):
    return jnp.dot(a, b, preferred_element_type=F32)


def three_parts(x):
    hi = x.astype(BF16).astype(F32)
    mid = (x - hi).astype(BF16).astype(F32)
    return hi, mid, x - hi - mid


def own_head():
    return lax.axis_index("mem")


def pack_kernel(
    heads, q_ref, k_ref, v_ref, gamma_ref, ids_ref, weights_ref, out_ref, rows_ref, sem, out_sem
):
    copies = []
    for h in range(heads):
        for at, ref in ((QA, k_ref), (QA + TOK, v_ref), (0, q_ref)):
            copies.append(
                pltpu.make_async_copy(
                    ref.at[:, h * HD : (h + 1) * HD],
                    rows_ref.at[h, at : at + TOK],
                    sem.at[len(copies)],
                )
            )
    for copy in copies:
        copy.start()
    ids = ids_ref[...]
    w_hi, w_mid, w_lo = three_parts(weights_ref[...])
    memory = iota((heads, TOK), 0)
    hit0, hit1 = memory == ids[0:1], memory == ids[1:2]
    hits = jnp.where(hit0 | hit1, 1.0, 0.0).astype(BF16)
    earlier = (iota((TOK, TOK), 0) < iota((TOK, TOK), 1)).astype(BF16)
    before = dot(hits, earlier)
    rank0 = jnp.sum(jnp.where(hit0, before, 0.0), axis=0, keepdims=True)
    rank1 = jnp.sum(jnp.where(hit1, before, 0.0), axis=0, keepdims=True)
    row = iota((AUX, TOK), 0)
    shared = jnp.zeros((AUX, TOK), F32)
    entries = [ids[0:1].astype(F32), rank0, ids[1:2].astype(F32), rank1]
    for part in (w_hi, w_mid, w_lo):
        entries += [part[0:1], part[1:2]]
    for at, entry in enumerate(entries):
        shared = jnp.where(row == at + 1, entry, shared)
    gamma_rows = gamma_ref[...].astype(F32)
    for h in range(heads):
        aux = jnp.where(row == 0, gamma_rows[h : h + 1], shared)
        rows_ref[h, TOK:QA] = aux.astype(BF16)
    leaving = []
    for h in range(heads):
        for copy in copies[3 * h : 3 * h + 3]:
            copy.wait()
        leaving.append(pltpu.make_async_copy(rows_ref.at[h], out_ref.at[h], out_sem.at[h]))
        leaving[h].start()
    for copy in leaving:
        copy.wait()


def head_rates(rate_ref, head, scratch_ref):
    rates = rate_ref[...].astype(F32)
    mine = jnp.where(iota(rates.shape, 1) == head, rates, 0.0)
    scratch_ref[...] = jnp.broadcast_to(jnp.sum(mine, axis=1, keepdims=True), scratch_ref.shape)


def slot_ids(aux, cap, side):
    at = aux[0:8].astype(jnp.int32)
    first = at[1:2] * (2 * cap) + at[2:3] + side * cap
    second = at[3:4] * (2 * cap) + at[4:5] + side * cap
    return first, second


def gather_kernel(
    cap, in_ref, rate_ref, slots_out, update_out, aux_ref, rows_ref, slots_ref, rest_ref, update_ref, rates_ref, later_ref, sem, aux_sem, slots_sem, update_sem
):
    sources = in_ref.shape[0]
    memories, slots, _ = slots_ref.shape
    width = memories * 2 * cap

    def arriving(source):
        return pltpu.make_async_copy(
            in_ref.at[source, QA : QA + 2 * TOK], rows_ref.at[source], sem.at[source]
        )

    small = pltpu.make_async_copy(in_ref.at[:, TOK:QA], aux_ref, aux_sem)
    small.start()
    for source in range(sources):
        arriving(source).start()
    head_rates(rate_ref, own_head(), rates_ref)
    after = (iota((TOK, TOK), 0) > iota((TOK, TOK), 1)).astype(BF16)
    memory = iota((memories, TOK), 0)
    small.wait()

    hits, gammas = [], []
    for source in range(sources):
        aux = aux_ref[source].astype(F32)
        at = aux.astype(jnp.int32)
        hit = (memory == at[1:2]) | (memory == at[3:4])
        gammas.append(jnp.where(hit, aux[0:1], 0.0))
    inside = dot(jnp.concatenate(gammas, axis=0).astype(BF16), after)
    behind = jnp.zeros((memories, 1), F32)
    for source in reversed(range(sources)):
        own = inside[source * memories : (source + 1) * memories]
        later_ref[source] = own + behind
        behind = behind + own[:, 0:1] + gammas[source][:, 0:1]
    total = -rates_ref[...] * behind

    place = iota((width, TOK), 0)

    def gather(pair, carry):
        rows, select, rest = [], [], jnp.zeros((width, TOK), F32)
        for side in range(2):
            source = 2 * pair + side
            arriving(source).wait()
            aux = aux_ref[source].astype(F32)
            at = aux.astype(jnp.int32)
            later = later_ref[source]
            rest0 = jnp.sum(jnp.where(memory == at[1:2], later, 0.0), axis=0, keepdims=True)
            rest1 = jnp.sum(jnp.where(memory == at[3:4], later, 0.0), axis=0, keepdims=True)
            first, second = slot_ids(aux, cap, side)
            hit0, hit1 = place == first, place == second
            select.append(jnp.where(hit0 | hit1, 1.0, 0.0).astype(BF16))
            rest = rest + jnp.where(hit0, rest0, jnp.where(hit1, rest1, 0.0))
            rows.append(
                jnp.concatenate([rows_ref[source, 0:TOK], rows_ref[source, TOK : 2 * TOK]], axis=1)
            )
        rest = jnp.broadcast_to(jnp.sum(rest, axis=1, keepdims=True), (width, HD))
        got = dot(jnp.concatenate(select, axis=1), jnp.concatenate(rows, axis=0)).astype(BF16)
        at = pl.ds(pl.multiple_of(pair * 2 * cap, 2 * cap), 2 * cap)
        for m in range(memories):
            slots_ref[m, at, :] = got[m * 2 * cap : (m + 1) * 2 * cap]
            rest_ref[m, at, :] = rest[m * 2 * cap : (m + 1) * 2 * cap]
        leaving(pair).start()
        return carry

    def leaving(pair):
        at = pl.ds(pl.multiple_of(pair * 2 * cap, 2 * cap), 2 * cap)
        return pltpu.make_async_copy(slots_ref.at[:, at], slots_out.at[:, at], slots_sem.at[pair])

    lax.fori_loop(0, sources // 2, gather, 0)

    row = iota((AUX, HD), 0)
    for m in range(memories):
        aux = jnp.zeros((AUX, HD), F32)
        for at, part in enumerate(three_parts(total[m : m + 1])):
            aux = jnp.where(row == at, part, aux)
        for half in range(2):
            update_ref[2 * m + half, PART_ROWS : PART_ROWS + AUX] = aux.astype(BF16)

    def updated(step):
        at = pl.ds(step * 8, 8)
        return pltpu.make_async_copy(update_ref.at[at], update_out.at[at], update_sem.at[step])

    def update(step, carry):
        for m in range(4):
            m = 4 * step + m
            k = slots_ref[m, :, 0:HD].astype(F32)
            v = slots_ref[m, :, HD : 2 * HD]
            kd = (k * jnp.exp(-rates_ref[pl.ds(m, 1), :] * rest_ref[m])).astype(BF16)
            added = tn(kd, v).astype(BF16)
            for half in range(2):
                part = added[half * PART_ROWS : (half + 1) * PART_ROWS]
                update_ref[2 * m + half, 0:PART_ROWS] = part
        updated(step).start()
        return carry

    lax.fori_loop(0, memories // 4, update, 0)
    for step in range(memories // 4):
        updated(step).wait()
    for pair in range(sources // 2):
        leaving(pair).wait()


def scan_kernel(in_ref, out_ref):
    state = jnp.zeros((PART_ROWS, HD), F32)
    for part in range(in_ref.shape[0]):
        out_ref[part] = state.astype(BF16)
        aux = in_ref[part, PART_ROWS : PART_ROWS + AUX].astype(F32)
        fade = jnp.exp(aux[0:1] + aux[1:2] + aux[2:3])
        state = fade * state + in_ref[part, 0:PART_ROWS].astype(F32)


def beside_kernel(
    cap,
    in_hbm,
    kv_hbm,
    rate_ref,
    raw_hbm,
    faded_hbm,
    pick_hbm,
    rows_ref,
    kv_ref,
    qg_ref,
    raw_ref,
    faded_ref,
    pick_ref,
    rates_ref,
    sums_ref,
    rows_sem,
    kv_sem,
    pick_sem,
    raw_sem,
    faded_sem,
):
    memories, slots, _ = kv_ref.shape
    pairs = pick_ref.shape[0]
    width = memories * 2 * cap

    def rows_in(pair):
        two = pl.ds(2 * pair, 2)
        return pltpu.make_async_copy(in_hbm.at[two, 0:QA], rows_ref.at[two], rows_sem.at[pair])

    def kv_in(step):
        four = pl.ds(4 * step, 4)
        return pltpu.make_async_copy(kv_hbm.at[four], kv_ref.at[four], kv_sem.at[step])

    def pick_out(pair):
        return pltpu.make_async_copy(pick_ref.at[pair], pick_hbm.at[pair], pick_sem.at[pair])

    def made_out(step):
        two = pl.ds(2 * step, 2)
        return (
            pltpu.make_async_copy(raw_ref.at[two], raw_hbm.at[two], raw_sem.at[step]),
            pltpu.make_async_copy(faded_ref.at[two], faded_hbm.at[two], faded_sem.at[step]),
        )

    for pair in range(pairs):
        rows_in(pair).start()
    for step in range(memories // 4):
        kv_in(step).start()
    head_rates(rate_ref, own_head(), rates_ref)
    tri = iota((TOK, TOK), 0) - iota((TOK, TOK), 1)
    sums_ref[0:TOK] = (tri >= 0).astype(BF16)
    sums_ref[TOK : 2 * TOK] = (tri < 0).astype(BF16)
    ones = jnp.ones((TOK, HD), BF16)
    eye = (tri == 0).astype(BF16)
    down, across = iota((width, TOK), 0), iota((TOK, width), 1)

    def route(pair, carry):
        rows_in(pair).wait()
        rows, select = [], []
        for side in range(2):
            packed = rows_ref[2 * pair + side, TOK:QA]
            aux = packed.astype(F32)
            gamma = dot(jnp.where(tri == 0, aux[0:1], 0.0).astype(BF16), ones).astype(BF16)
            rows.append(jnp.concatenate([rows_ref[2 * pair + side, 0:TOK], gamma], axis=1))
            first, second = slot_ids(aux, cap, side)
            hit = (down == first) | (down == second)
            select.append(jnp.where(hit, 1.0, 0.0).astype(BF16))
            aux = nt(eye, packed)
            at = aux.astype(jnp.int32)
            first = at[:, 1:2] * (2 * cap) + at[:, 2:3] + side * cap
            second = at[:, 3:4] * (2 * cap) + at[:, 4:5] + side * cap
            w0 = aux[:, 5:6] + aux[:, 7:8] + aux[:, 9:10]
            w1 = aux[:, 6:7] + aux[:, 8:9] + aux[:, 10:11]
            pick = jnp.where(across == first, w0, jnp.where(across == second, w1, 0.0))
            pick_ref[pair, side * TOK : (side + 1) * TOK] = pick.astype(BF16)
        pick_out(pair).start()
        got = dot(jnp.concatenate(select, axis=1), jnp.concatenate(rows, axis=0)).astype(BF16)
        at = pl.ds(pl.multiple_of(pair * 2 * cap, 2 * cap), 2 * cap)
        for m in range(memories):
            qg_ref[m, at, :] = got[m * 2 * cap : (m + 1) * 2 * cap]
        return carry

    lax.fori_loop(0, pairs, route, 0, unroll=1)
    for step in range(memories // 4):
        kv_in(step).wait()

    def intra(step, carry):
        for m in (2 * step, 2 * step + 1):
            rate = rates_ref[pl.ds(m, 1), :]
            behind = []
            faded_all = jnp.ones((1, HD), F32)
            for b in range(slots // TOK):
                at = slice(b * TOK, (b + 1) * TOK)
                seen = slice(0, (b + 1) * TOK)
                q = qg_ref[m, at, 0:HD]
                gamma = qg_ref[m, at, HD : 2 * HD]
                masked = jnp.where(tri > 0, gamma.astype(F32), 0.0).astype(BF16)
                sums = dot(sums_ref[...], jnp.concatenate([masked, gamma], axis=1))
                inside = jnp.where(tri >= 0, jnp.exp(-rate * sums[0:TOK, 0:TOK]), 0.0)
                fade = jnp.exp(-rate * sums[0:TOK, TOK : 2 * TOK])
                faded_ref[m, at] = (q.astype(F32) * (fade * faded_all)).astype(BF16)
                decay = jnp.concatenate([fade * row for row in behind] + [inside], axis=1)
                weights = (decay * nt(q, kv_ref[m, seen, 0:HD])).astype(BF16)
                raw_ref[m, at] = dot(weights, kv_ref[m, seen, HD : 2 * HD])
                if (b + 1) * TOK < slots:
                    whole = fade[TOK - 1 : TOK]
                    faded_all = faded_all * whole
                    rest = jnp.exp(-rate * sums[TOK : 2 * TOK, TOK : 2 * TOK])
                    behind = [row * whole for row in behind] + [rest.T]
        for copy in made_out(step):
            copy.start()
        return carry

    lax.fori_loop(0, memories // 2, intra, 0, unroll=1)
    for pair in range(pairs):
        pick_out(pair).wait()
    for step in range(memories // 2):
        for copy in made_out(step):
            copy.wait()


def finish_kernel(cap, faded_ref, raw_ref, pick_ref, state_ref, gain_ref, out_ref, made_ref):
    memories = faded_ref.shape[0]

    def one(m, carry):
        raw = raw_ref[m] + dot(faded_ref[m], state_ref[m])
        mean = jnp.mean(raw * raw, axis=1, keepdims=True)
        made_ref[m] = (raw * lax.rsqrt(mean + EPS)).astype(BF16)
        return carry

    lax.fori_loop(0, memories, one, 0, unroll=4)
    gain = gain_ref[pl.ds(own_head(), 1), :]

    def mix(pair, carry):
        at = pl.ds(pl.multiple_of(pair * 2 * cap, 2 * cap), 2 * cap)
        rows = jnp.concatenate([made_ref[m, at, :] for m in range(memories)], axis=0)
        mixed = (gain * dot(pick_ref[pair], rows)).astype(BF16)
        for side in range(2):
            out_ref[2 * pair + side] = mixed[side * TOK : (side + 1) * TOK]
        return carry

    lax.fori_loop(0, pick_ref.shape[0], mix, 0, unroll=4)


def unpack_kernel(in_ref, out_ref):
    for h in range(in_ref.shape[0]):
        out_ref[:, h * HD : (h + 1) * HD] = in_ref[h]


like = jax.ShapeDtypeStruct
ANY = pl.BlockSpec(memory_space=pl.ANY)
WHOLE = pl.BlockSpec(memory_space=pltpu.VMEM)
DMA = pltpu.SemaphoreType.DMA


def call(kernel, outs, ins, out_specs, room, scratch=(), grid=(), flops=0, moved=0):
    return pl.pallas_call(
        kernel,
        out_shape=outs,
        grid=grid,
        in_specs=ins,
        out_specs=out_specs,
        scratch_shapes=list(scratch),
        compiler_params=pltpu.CompilerParams(vmem_limit_bytes=VMEM_ALL - room),
        cost_estimate=pl.CostEstimate(flops=flops, bytes_accessed=moved, transcendentals=0),
    )


def pack(heads):
    return call(
        lambda *refs: pack_kernel(heads, *refs),
        like((heads, QA + 2 * TOK, HD), BF16),
        [ANY, ANY, ANY, WHOLE, WHOLE, WHOLE],
        ANY,
        -2_000_000,
        (
            pltpu.VMEM((heads, QA + 2 * TOK, HD), BF16),
            DMA((3 * heads,)),
            DMA((heads,)),
        ),
    )


def gather(memories, sources, parts):
    cap = 3 * TOK // memories
    slots = sources * cap
    return call(
        lambda *refs: gather_kernel(cap, *refs),
        (
            like((memories, slots, 2 * HD), BF16),
            like((parts, PART_ROWS + AUX, HD), BF16),
        ),
        [ANY, WHOLE],
        (ANY, ANY),
        -2_000_000,
        (
            pltpu.VMEM((sources, AUX, TOK), BF16),
            pltpu.VMEM((sources, 2 * TOK, HD), BF16),
            pltpu.VMEM((memories, slots, 2 * HD), BF16),
            pltpu.VMEM((memories, slots, HD), F32),
            pltpu.VMEM((parts, PART_ROWS + AUX, HD), BF16),
            pltpu.VMEM((memories, HD), F32),
            pltpu.VMEM((sources, memories, TOK), F32),
            DMA((sources,)),
            DMA(()),
            DMA((sources // 2,)),
            DMA((memories // 4,)),
        ),
    )


def scan(parts):
    return call(
        scan_kernel,
        like((parts, PART_ROWS, HD), BF16),
        [WHOLE],
        WHOLE,
        40_000_000,
        flops=2 * 10**10,
        moved=2**20,
    )


def beside(memories, sources):
    cap = 3 * TOK // memories
    slots = sources * cap
    pairs = sources // 2
    pick = (pairs, 2 * TOK, memories * 2 * cap)
    return call(
        lambda *refs: beside_kernel(cap, *refs),
        (like((memories, slots, HD), F32), like((memories, slots, HD), BF16), like(pick, BF16)),
        [ANY, ANY, WHOLE],
        (ANY, ANY, ANY),
        -2_000_000,
        (
            pltpu.VMEM((sources, QA, HD), BF16),
            pltpu.VMEM((memories, slots, 2 * HD), BF16),
            pltpu.VMEM((memories, slots, 2 * HD), BF16),
            pltpu.VMEM((memories, slots, HD), F32),
            pltpu.VMEM((memories, slots, HD), BF16),
            pltpu.VMEM(pick, BF16),
            pltpu.VMEM((memories, HD), F32),
            pltpu.VMEM((2 * TOK, TOK), BF16),
            DMA((pairs,)),
            DMA((memories // 4,)),
            DMA((pairs,)),
            DMA((memories // 2,)),
            DMA((memories // 2,)),
        ),
        flops=15 * 10**9,
        moved=12 * 2**20,
    )


def finish(memories, sources):
    cap = 3 * TOK // memories
    slots = sources * cap
    return call(
        lambda *refs: finish_kernel(cap, *refs),
        like((sources, TOK, HD), BF16),
        [WHOLE] * 5,
        WHOLE,
        40_000_000,
        (pltpu.VMEM((memories, slots, HD), BF16),),
    )


def unpack(heads):
    return call(unpack_kernel, like((TOK, heads * HD), BF16), [WHOLE], WHOLE, 40_000_000)


def body(queries, keys, values, gamma, rate, route_ids, route_weights, norm_gain):
    heads = gamma.shape[1]
    memories = rate.shape[0]
    sources = lax.axis_size("mem")
    parts = lax.axis_size("seq")
    send = pack(heads)(queries, keys, values, gamma.T, route_ids.T, route_weights.T)
    arrived = lax.all_to_all(send, "mem", 0, 0, tiled=True)
    slot_rows, update = gather(memories, sources, parts)(arrived, rate)
    pieces = lax.all_to_all(update, "seq", 0, 0, tiled=True)
    raw, faded, pick = beside(memories, sources)(arrived, slot_rows, rate)
    pieces, raw, faded, pick = lax.optimization_barrier((pieces, raw, faded, pick))
    before = scan(parts)(pieces)
    state = lax.all_to_all(before, "seq", 0, 0, tiled=True).reshape(memories, HD, HD)
    gain = norm_gain.reshape(heads, HD)
    mixed = finish(memories, sources)(faded, raw, pick, state, gain)
    returned = lax.all_to_all(mixed, "mem", 0, 0, tiled=True)
    return unpack(heads)(returned)


def solution(mesh):
    split = P(("seq", "mem"), None)
    return jax.shard_map(
        body,
        mesh=mesh,
        in_specs=(split, split, split, split, P(), split, split, P()),
        out_specs=split,
        check_vma=False,
    )
```

```python
import jax
import jax.numpy as jnp
from jax import lax
from jax.experimental import pallas as pl
from jax.experimental.pallas import tpu as pltpu
from jax.sharding import PartitionSpec as P

F32, BF16 = jnp.float32, jnp.bfloat16
TOK = 128
HD = 128
AUX = 16
QA = TOK + AUX
PART_ROWS = 64
GROUPS = 2
EPS = 1e-6
VMEM_ALL = 58_000_000
ROOM = 4_900_000


def iota(shape, dim):
    return lax.broadcasted_iota(jnp.int32, shape, dim)


def nt(a, b):
    return lax.dot_general(a, b, (((1,), (1,)), ((), ())), preferred_element_type=F32)


def tn(a, b):
    return lax.dot_general(a, b, (((0,), (0,)), ((), ())), preferred_element_type=F32)


def dot(a, b):
    return jnp.dot(a, b, preferred_element_type=F32)


def three_parts(x):
    hi = x.astype(BF16).astype(F32)
    mid = (x - hi).astype(BF16).astype(F32)
    return hi, mid, x - hi - mid


def own_head():
    return lax.axis_index("mem")


def pack_kernel(
    heads, q_ref, k_ref, v_ref, gamma_hbm, ids_hbm, weights_hbm, out_ref, gamma_ref, ids_ref, weights_ref, given_ref, rows_ref, small_sem, sem, out_sem
):
    groups, lanes = out_sem.shape[0], heads * HD // out_sem.shape[0]

    def arriving(group):
        at = slice(group * lanes, (group + 1) * lanes)
        return [
            pltpu.make_async_copy(ref.at[:, at], given_ref.at[which, :, at], sem.at[which, group])
            for which, ref in enumerate((q_ref, k_ref, v_ref))
        ]

    small = [
        pltpu.make_async_copy(gamma_hbm, gamma_ref, small_sem.at[0]),
        pltpu.make_async_copy(ids_hbm, ids_ref, small_sem.at[1]),
        pltpu.make_async_copy(weights_hbm, weights_ref, small_sem.at[2]),
    ]
    for copy in small:
        copy.start()
    for group in range(groups):
        for copy in arriving(group):
            copy.start()
    for copy in small:
        copy.wait()
    ids = ids_ref[...]
    w_hi, w_mid, w_lo = three_parts(weights_ref[...])
    memory = iota((heads, TOK), 0)
    hit0, hit1 = memory == ids[0:1], memory == ids[1:2]
    hits = jnp.where(hit0 | hit1, 1.0, 0.0).astype(BF16)
    earlier = (iota((TOK, TOK), 0) < iota((TOK, TOK), 1)).astype(BF16)
    before = dot(hits, earlier)
    rank0 = jnp.sum(jnp.where(hit0, before, 0.0), axis=0, keepdims=True)
    rank1 = jnp.sum(jnp.where(hit1, before, 0.0), axis=0, keepdims=True)
    row = iota((AUX, TOK), 0)
    shared = jnp.zeros((AUX, TOK), F32)
    entries = [ids[0:1].astype(F32), rank0, ids[1:2].astype(F32), rank1]
    for part in (w_hi, w_mid, w_lo):
        entries += [part[0:1], part[1:2]]
    for at, entry in enumerate(entries):
        shared = jnp.where(row == at + 1, entry, shared)
    gamma_rows = gamma_ref[...].astype(F32)
    for h in range(heads):
        aux = jnp.where(row == 0, gamma_rows[h : h + 1], shared)
        rows_ref[h, TOK:QA] = aux.astype(BF16)
    leaving = []
    for group in range(groups):
        for copy in arriving(group):
            copy.wait()
        some = range(group * heads // groups, (group + 1) * heads // groups)
        for h in some:
            for which, at in enumerate((0, QA, QA + TOK)):
                rows_ref[h, at : at + TOK] = given_ref[which, :, h * HD : (h + 1) * HD]
        at = pl.ds(some[0], len(some))
        leaving.append(pltpu.make_async_copy(rows_ref.at[at], out_ref.at[at], out_sem.at[group]))
        leaving[group].start()
    for copy in leaving:
        copy.wait()


def head_rates(rate_ref, head, scratch_ref):
    rates = rate_ref[...].astype(F32)
    mine = jnp.where(iota(rates.shape, 1) == head, rates, 0.0)
    scratch_ref[...] = jnp.broadcast_to(jnp.sum(mine, axis=1, keepdims=True), scratch_ref.shape)


def own_slots(aux, cap):
    at = aux[0:8].astype(jnp.int32)
    return at[1:2] * cap + at[2:3], at[3:4] * cap + at[4:5]


def spread(rows, cap, side):
    parts = rows.reshape(-1, cap, rows.shape[1])
    parts = [parts, jnp.zeros_like(parts)][:: 1 - 2 * side]
    return jnp.concatenate(parts, axis=1).reshape(-1, rows.shape[1])


def gather_kernel(
    cap, in_ref, rate_ref, slots_out, update_out, slots_ref, rest_ref, update_ref, rates_ref, later_ref, slots_sem, update_sem
):
    sources = in_ref.shape[0]
    memories, slots, _ = slots_ref.shape
    width = memories * 2 * cap

    head_rates(rate_ref, own_head(), rates_ref)
    after = (iota((TOK, TOK), 0) > iota((TOK, TOK), 1)).astype(BF16)
    memory = iota((memories, TOK), 0)
    hits, gammas = [], []
    for source in range(sources):
        aux = in_ref[source, TOK:QA].astype(F32)
        at = aux.astype(jnp.int32)
        hit = (memory == at[1:2]) | (memory == at[3:4])
        gammas.append(jnp.where(hit, aux[0:1], 0.0))
    inside = dot(jnp.concatenate(gammas, axis=0).astype(BF16), after)
    behind = jnp.zeros((memories, 1), F32)
    for source in reversed(range(sources)):
        own = inside[source * memories : (source + 1) * memories]
        later_ref[source] = own + behind
        behind = behind + own[:, 0:1] + gammas[source][:, 0:1]
    total = -rates_ref[...] * behind

    place = iota((width // 2, TOK), 0)

    def gather(pair, carry):
        rows, select, rest = [], [], []
        for side in range(2):
            source = 2 * pair + side
            aux = in_ref[source, TOK:QA].astype(F32)
            at = aux.astype(jnp.int32)
            later = later_ref[source]
            rest0 = jnp.sum(jnp.where(memory == at[1:2], later, 0.0), axis=0, keepdims=True)
            rest1 = jnp.sum(jnp.where(memory == at[3:4], later, 0.0), axis=0, keepdims=True)
            first, second = own_slots(aux, cap)
            hit0, hit1 = place == first, place == second
            select.append(spread(jnp.where(hit0 | hit1, 1.0, 0.0), cap, side).astype(BF16))
            own = jnp.where(hit0, rest0, jnp.where(hit1, rest1, 0.0))
            own = jnp.broadcast_to(jnp.sum(own, axis=1, keepdims=True), own.shape)
            rest.append(own.reshape(memories, cap, TOK))
            k, v = in_ref[source, QA : QA + TOK], in_ref[source, QA + TOK : QA + 2 * TOK]
            rows.append(jnp.concatenate([k, v], axis=1))
        rest = jnp.concatenate(rest, axis=1)
        got = dot(jnp.concatenate(select, axis=1), jnp.concatenate(rows, axis=0)).astype(BF16)
        at = pl.ds(pl.multiple_of(pair * 2 * cap, 2 * cap), 2 * cap)
        for m in range(memories):
            slots_ref[m, at, :] = got[m * 2 * cap : (m + 1) * 2 * cap]
            rest_ref[m, at, :] = rest[m]
        leaving(pair).start()
        return carry

    def leaving(pair):
        at = pl.ds(pl.multiple_of(pair * 2 * cap, 2 * cap), 2 * cap)
        return pltpu.make_async_copy(slots_ref.at[:, at], slots_out.at[:, at], slots_sem.at[pair])

    lax.fori_loop(0, sources // 2, gather, 0, unroll=2)

    row = iota((AUX, HD), 0)
    for m in range(memories):
        aux = jnp.zeros((AUX, HD), F32)
        for at, part in enumerate(three_parts(total[m : m + 1])):
            aux = jnp.where(row == at, part, aux)
        for half in range(2):
            update_ref[2 * m + half, PART_ROWS : PART_ROWS + AUX] = aux.astype(BF16)

    def updated(step):
        at = pl.ds(step * 8, 8)
        return pltpu.make_async_copy(update_ref.at[at], update_out.at[at], update_sem.at[step])

    def update(step, carry):
        for m in range(4):
            m = 4 * step + m
            k = slots_ref[m, :, 0:HD].astype(F32)
            v = slots_ref[m, :, HD : 2 * HD]
            kd = (k * jnp.exp(-rates_ref[pl.ds(m, 1), :] * rest_ref[m])).astype(BF16)
            added = tn(kd, v).astype(BF16)
            for half in range(2):
                part = added[half * PART_ROWS : (half + 1) * PART_ROWS]
                update_ref[2 * m + half, 0:PART_ROWS] = part
        updated(step).start()
        return carry

    lax.fori_loop(0, memories // 4, update, 0)
    for step in range(memories // 4):
        updated(step).wait()
    for pair in range(sources // 2):
        leaving(pair).wait()


def scan_kernel(in_ref, out_ref):
    state = jnp.zeros((PART_ROWS, HD), F32)
    for part in range(in_ref.shape[0]):
        out_ref[part] = state.astype(BF16)
        aux = in_ref[part, PART_ROWS : PART_ROWS + AUX].astype(F32)
        fade = jnp.exp(aux[0:1] + aux[1:2] + aux[2:3])
        state = fade * state + in_ref[part, 0:PART_ROWS].astype(F32)


def beside_kernel(
    cap,
    in_ref,
    kv_hbm,
    rate_ref,
    raw_hbm,
    faded_hbm,
    pick_hbm,
    kv_ref,
    qg_ref,
    raw_ref,
    faded_ref,
    pick_ref,
    rates_ref,
    sums_ref,
    kv_sem,
    pick_sem,
    raw_sem,
    faded_sem,
):
    memories, slots, _ = kv_ref.shape
    pairs = pick_ref.shape[0]
    width = memories * 2 * cap

    def kv_in(step):
        four = pl.ds(4 * step, 4)
        return pltpu.make_async_copy(kv_hbm.at[four], kv_ref.at[four], kv_sem.at[step])

    def pick_out(pair):
        return pltpu.make_async_copy(pick_ref.at[pair], pick_hbm.at[pair], pick_sem.at[pair])

    def made_out(step):
        two = pl.ds(2 * step, 2)
        return (
            pltpu.make_async_copy(raw_ref.at[two], raw_hbm.at[two], raw_sem.at[step]),
            pltpu.make_async_copy(faded_ref.at[two], faded_hbm.at[two], faded_sem.at[step]),
        )

    for step in range(memories // 4):
        kv_in(step).start()
    head_rates(rate_ref, own_head(), rates_ref)
    tri = iota((TOK, TOK), 0) - iota((TOK, TOK), 1)
    sums_ref[0:TOK] = (tri >= 0).astype(BF16)
    sums_ref[TOK : 2 * TOK] = (tri < 0).astype(BF16)
    ones = jnp.ones((TOK, HD), BF16)
    eye = (tri == 0).astype(BF16)
    down, across = iota((width // 2, TOK), 0), iota((TOK, width), 1)

    def route(pair, carry):
        rows, select = [], []
        for side in range(2):
            packed = in_ref[2 * pair + side, TOK:QA]
            aux = packed.astype(F32)
            gamma = dot(jnp.where(tri == 0, aux[0:1], 0.0).astype(BF16), ones).astype(BF16)
            rows.append(jnp.concatenate([in_ref[2 * pair + side, 0:TOK], gamma], axis=1))
            first, second = own_slots(aux, cap)
            hit = (down == first) | (down == second)
            select.append(spread(jnp.where(hit, 1.0, 0.0), cap, side).astype(BF16))
            aux = nt(eye, packed)
            at = aux.astype(jnp.int32)
            first = at[:, 1:2] * (2 * cap) + at[:, 2:3] + side * cap
            second = at[:, 3:4] * (2 * cap) + at[:, 4:5] + side * cap
            w0 = aux[:, 5:6] + aux[:, 7:8] + aux[:, 9:10]
            w1 = aux[:, 6:7] + aux[:, 8:9] + aux[:, 10:11]
            pick = jnp.where(across == first, w0, jnp.where(across == second, w1, 0.0))
            pick_ref[pair, side * TOK : (side + 1) * TOK] = pick.astype(BF16)
        pick_out(pair).start()
        got = dot(jnp.concatenate(select, axis=1), jnp.concatenate(rows, axis=0)).astype(BF16)
        at = pl.ds(pl.multiple_of(pair * 2 * cap, 2 * cap), 2 * cap)
        for m in range(memories):
            qg_ref[m, at, :] = got[m * 2 * cap : (m + 1) * 2 * cap]
        return carry

    lax.fori_loop(0, pairs, route, 0)
    for step in range(memories // 4):
        kv_in(step).wait()

    def intra(step, carry):
        for m in (2 * step, 2 * step + 1):
            rate = rates_ref[pl.ds(m, 1), :]
            behind = []
            faded_all = jnp.ones((1, HD), F32)
            for b in range(slots // TOK):
                at = slice(b * TOK, (b + 1) * TOK)
                seen = slice(0, (b + 1) * TOK)
                q = qg_ref[m, at, 0:HD]
                gamma = qg_ref[m, at, HD : 2 * HD]
                masked = jnp.where(tri > 0, gamma.astype(F32), 0.0).astype(BF16)
                sums = dot(sums_ref[...], jnp.concatenate([masked, gamma], axis=1))
                inside = jnp.where(tri >= 0, jnp.exp(-rate * sums[0:TOK, 0:TOK]), 0.0)
                fade = jnp.exp(-rate * sums[0:TOK, TOK : 2 * TOK])
                faded_ref[m, at] = (q.astype(F32) * (fade * faded_all)).astype(BF16)
                decay = jnp.concatenate([fade * row for row in behind] + [inside], axis=1)
                weights = (decay * nt(q, kv_ref[m, seen, 0:HD])).astype(BF16)
                raw_ref[m, at] = dot(weights, kv_ref[m, seen, HD : 2 * HD])
                if (b + 1) * TOK < slots:
                    whole = fade[TOK - 1 : TOK]
                    faded_all = faded_all * whole
                    rest = jnp.exp(-rate * sums[TOK : 2 * TOK, TOK : 2 * TOK])
                    behind = [row * whole for row in behind] + [rest.T]
        for copy in made_out(step):
            copy.start()
        return carry

    lax.fori_loop(0, memories // 2, intra, 0, unroll=2)
    for pair in range(pairs):
        pick_out(pair).wait()
    for step in range(memories // 2):
        for copy in made_out(step):
            copy.wait()


def finish_kernel(cap, faded_ref, raw_ref, pick_ref, state_ref, gain_ref, out_ref, made_ref):
    memories = faded_ref.shape[0]

    def one(m, carry):
        raw = raw_ref[m] + dot(faded_ref[m], state_ref[m])
        mean = jnp.mean(raw * raw, axis=1, keepdims=True)
        made_ref[m] = (raw * lax.rsqrt(mean + EPS)).astype(BF16)
        return carry

    lax.fori_loop(0, memories, one, 0, unroll=4)
    gain = gain_ref[pl.ds(own_head(), 1), :]

    def mix(pair, carry):
        at = pl.ds(pl.multiple_of(pair * 2 * cap, 2 * cap), 2 * cap)
        rows = jnp.concatenate([made_ref[m, at, :] for m in range(memories)], axis=0)
        mixed = (gain * dot(pick_ref[pair], rows)).astype(BF16)
        for side in range(2):
            out_ref[2 * pair + side] = mixed[side * TOK : (side + 1) * TOK]
        return carry

    lax.fori_loop(0, pick_ref.shape[0], mix, 0, unroll=4)


def unpack_kernel(in_ref, out_ref):
    for h in range(in_ref.shape[0]):
        out_ref[:, h * HD : (h + 1) * HD] = in_ref[h]


like = jax.ShapeDtypeStruct
ANY = pl.BlockSpec(memory_space=pl.ANY)
WHOLE = pl.BlockSpec(memory_space=pltpu.VMEM)
DMA = pltpu.SemaphoreType.DMA


def call(kernel, outs, ins, out_specs, room, scratch=(), grid=(), flops=0, moved=0):
    return pl.pallas_call(
        kernel,
        out_shape=outs,
        grid=grid,
        in_specs=ins,
        out_specs=out_specs,
        scratch_shapes=list(scratch),
        compiler_params=pltpu.CompilerParams(vmem_limit_bytes=VMEM_ALL - room),
        cost_estimate=pl.CostEstimate(flops=flops, bytes_accessed=moved, transcendentals=0),
    )


def pack(heads):
    return call(
        lambda *refs: pack_kernel(heads, *refs),
        like((heads, QA + 2 * TOK, HD), BF16),
        [ANY] * 6,
        ANY,
        -2_000_000,
        (
            pltpu.VMEM((heads, TOK), BF16),
            pltpu.VMEM((2, TOK), jnp.int32),
            pltpu.VMEM((2, TOK), F32),
            pltpu.VMEM((3, TOK, heads * HD), BF16),
            pltpu.VMEM((heads, QA + 2 * TOK, HD), BF16),
            DMA((3,)),
            DMA((3, GROUPS)),
            DMA((GROUPS,)),
        ),
    )


def gather(memories, sources, parts):
    cap = 3 * TOK // memories
    slots = sources * cap
    return call(
        lambda *refs: gather_kernel(cap, *refs),
        (
            like((memories, slots, 2 * HD), BF16),
            like((parts, PART_ROWS + AUX, HD), BF16),
        ),
        [WHOLE, WHOLE],
        (ANY, ANY),
        ROOM,
        (
            pltpu.VMEM((memories, slots, 2 * HD), BF16),
            pltpu.VMEM((memories, slots, HD), F32),
            pltpu.VMEM((parts, PART_ROWS + AUX, HD), BF16),
            pltpu.VMEM((memories, HD), F32),
            pltpu.VMEM((sources, memories, TOK), F32),
            DMA((sources // 2,)),
            DMA((memories // 4,)),
        ),
    )


def scan(parts):
    return call(
        scan_kernel,
        like((parts, PART_ROWS, HD), BF16),
        [WHOLE],
        WHOLE,
        40_000_000,
        flops=2 * 10**10,
        moved=2**20,
    )


def beside(memories, sources):
    cap = 3 * TOK // memories
    slots = sources * cap
    pairs = sources // 2
    pick = (pairs, 2 * TOK, memories * 2 * cap)
    return call(
        lambda *refs: beside_kernel(cap, *refs),
        (like((memories, slots, HD), F32), like((memories, slots, HD), BF16), like(pick, BF16)),
        [WHOLE, ANY, WHOLE],
        (ANY, ANY, ANY),
        ROOM,
        (
            pltpu.VMEM((memories, slots, 2 * HD), BF16),
            pltpu.VMEM((memories, slots, 2 * HD), BF16),
            pltpu.VMEM((memories, slots, HD), F32),
            pltpu.VMEM((memories, slots, HD), BF16),
            pltpu.VMEM(pick, BF16),
            pltpu.VMEM((memories, HD), F32),
            pltpu.VMEM((2 * TOK, TOK), BF16),
            DMA((memories // 4,)),
            DMA((pairs,)),
            DMA((memories // 2,)),
            DMA((memories // 2,)),
        ),
        flops=15 * 10**9,
        moved=12 * 2**20,
    )


def finish(memories, sources):
    cap = 3 * TOK // memories
    slots = sources * cap
    return call(
        lambda *refs: finish_kernel(cap, *refs),
        like((sources, TOK, HD), BF16),
        [WHOLE] * 5,
        WHOLE,
        40_000_000,
        (pltpu.VMEM((memories, slots, HD), BF16),),
    )


def unpack(heads):
    return call(unpack_kernel, like((TOK, heads * HD), BF16), [WHOLE], WHOLE, 40_000_000)


def body(queries, keys, values, gamma, rate, route_ids, route_weights, norm_gain):
    heads = gamma.shape[1]
    memories = rate.shape[0]
    sources = lax.axis_size("mem")
    parts = lax.axis_size("seq")
    send = pack(heads)(queries, keys, values, gamma.T, route_ids.T, route_weights.T)
    arrived = lax.all_to_all(send, "mem", 0, 0, tiled=True)
    slot_rows, update = gather(memories, sources, parts)(arrived, rate)
    pieces = lax.all_to_all(update, "seq", 0, 0, tiled=True)
    raw, faded, pick = beside(memories, sources)(arrived, slot_rows, rate)
    pieces, raw, faded, pick = lax.optimization_barrier((pieces, raw, faded, pick))
    before = scan(parts)(pieces)
    state = lax.all_to_all(before, "seq", 0, 0, tiled=True).reshape(memories, HD, HD)
    gain = norm_gain.reshape(heads, HD)
    mixed = finish(memories, sources)(faded, raw, pick, state, gain)
    returned = lax.all_to_all(mixed, "mem", 0, 0, tiled=True)
    return unpack(heads)(returned)


def solution(mesh):
    split = P(("seq", "mem"), None)
    return jax.shard_map(
        body,
        mesh=mesh,
        in_specs=(split, split, split, split, P(), split, split, P()),
        out_specs=split,
        check_vma=False,
    )
```

```python
import jax
import jax.numpy as jnp
from jax import lax
from jax.experimental import pallas as pl
from jax.experimental.pallas import tpu as pltpu
from jax.sharding import PartitionSpec as P

F32, BF16 = jnp.float32, jnp.bfloat16
TOK = 128
HD = 128
AUX = 16
QA = TOK + AUX
PART_ROWS = 64
GROUPS = 2
EPS = 1e-6
VMEM_ALL = 58_000_000
ROOM = 4_200_000


def iota(shape, dim):
    return lax.broadcasted_iota(jnp.int32, shape, dim)


def nt(a, b):
    return lax.dot_general(a, b, (((1,), (1,)), ((), ())), preferred_element_type=F32)


def tn(a, b):
    return lax.dot_general(a, b, (((0,), (0,)), ((), ())), preferred_element_type=F32)


def dot(a, b):
    return jnp.dot(a, b, preferred_element_type=F32)


def three_parts(x):
    hi = x.astype(BF16).astype(F32)
    mid = (x - hi).astype(BF16).astype(F32)
    return hi, mid, x - hi - mid


def own_head():
    return lax.axis_index("mem")


def pack_kernel(
    heads, q_ref, k_ref, v_ref, gamma_hbm, ids_hbm, weights_hbm, out_ref, gamma_ref, ids_ref, weights_ref, given_ref, rows_ref, small_sem, sem, out_sem
):
    groups, lanes = out_sem.shape[0], heads * HD // out_sem.shape[0]

    def arriving(group):
        at = slice(group * lanes, (group + 1) * lanes)
        return [
            pltpu.make_async_copy(ref.at[:, at], given_ref.at[which, :, at], sem.at[which, group])
            for which, ref in enumerate((q_ref, k_ref, v_ref))
        ]

    small = [
        pltpu.make_async_copy(gamma_hbm, gamma_ref, small_sem.at[0]),
        pltpu.make_async_copy(ids_hbm, ids_ref, small_sem.at[1]),
        pltpu.make_async_copy(weights_hbm, weights_ref, small_sem.at[2]),
    ]
    for copy in small:
        copy.start()
    for group in range(groups):
        for copy in arriving(group):
            copy.start()
    for copy in small:
        copy.wait()
    ids = ids_ref[...]
    w_hi, w_mid, w_lo = three_parts(weights_ref[...])
    memory = iota((heads, TOK), 0)
    hit0, hit1 = memory == ids[0:1], memory == ids[1:2]
    hits = jnp.where(hit0 | hit1, 1.0, 0.0).astype(BF16)
    earlier = (iota((TOK, TOK), 0) < iota((TOK, TOK), 1)).astype(BF16)
    before = dot(hits, earlier)
    rank0 = jnp.sum(jnp.where(hit0, before, 0.0), axis=0, keepdims=True)
    rank1 = jnp.sum(jnp.where(hit1, before, 0.0), axis=0, keepdims=True)
    row = iota((AUX, TOK), 0)
    shared = jnp.zeros((AUX, TOK), F32)
    entries = [ids[0:1].astype(F32), rank0, ids[1:2].astype(F32), rank1]
    for part in (w_hi, w_mid, w_lo):
        entries += [part[0:1], part[1:2]]
    for at, entry in enumerate(entries):
        shared = jnp.where(row == at + 1, entry, shared)
    gamma_rows = gamma_ref[...].astype(F32)
    for h in range(heads):
        aux = jnp.where(row == 0, gamma_rows[h : h + 1], shared)
        rows_ref[h, TOK:QA] = aux.astype(BF16)
    leaving = []
    for group in range(groups):
        for copy in arriving(group):
            copy.wait()
        some = range(group * heads // groups, (group + 1) * heads // groups)
        for h in some:
            for which, at in enumerate((0, QA, QA + TOK)):
                rows_ref[h, at : at + TOK] = given_ref[which, :, h * HD : (h + 1) * HD]
        at = pl.ds(some[0], len(some))
        leaving.append(pltpu.make_async_copy(rows_ref.at[at], out_ref.at[at], out_sem.at[group]))
        leaving[group].start()
    for copy in leaving:
        copy.wait()


def head_rates(rate_ref, head, scratch_ref):
    rates = rate_ref[...].astype(F32)
    mine = jnp.where(iota(rates.shape, 1) == head, rates, 0.0)
    scratch_ref[...] = jnp.broadcast_to(jnp.sum(mine, axis=1, keepdims=True), scratch_ref.shape)


def own_slots(aux, cap):
    at = aux[0:8].astype(jnp.int32)
    return at[1:2] * cap + at[2:3], at[3:4] * cap + at[4:5]


def spread(rows, cap, side):
    parts = rows.reshape(-1, cap, rows.shape[1])
    parts = [parts, jnp.zeros_like(parts)][:: 1 - 2 * side]
    return jnp.concatenate(parts, axis=1).reshape(-1, rows.shape[1])


def gather_kernel(
    cap, in_ref, rate_ref, slots_out, update_out, slots_ref, rest_ref, update_ref, rates_ref, later_ref, slots_sem, update_sem
):
    sources = in_ref.shape[0]
    memories, slots, _ = slots_ref.shape
    width = memories * 2 * cap

    head_rates(rate_ref, own_head(), rates_ref)
    after = (iota((TOK, TOK), 0) > iota((TOK, TOK), 1)).astype(BF16)
    memory = iota((memories, TOK), 0)
    hits, gammas = [], []
    for source in range(sources):
        aux = in_ref[source, TOK:QA].astype(F32)
        at = aux.astype(jnp.int32)
        hit = (memory == at[1:2]) | (memory == at[3:4])
        gammas.append(jnp.where(hit, aux[0:1], 0.0))
    inside = dot(jnp.concatenate(gammas, axis=0).astype(BF16), after)
    behind = jnp.zeros((memories, 1), F32)
    for source in reversed(range(sources)):
        own = inside[source * memories : (source + 1) * memories]
        later_ref[source] = own + behind
        behind = behind + own[:, 0:1] + gammas[source][:, 0:1]
    total = -rates_ref[...] * behind

    place = iota((width // 2, TOK), 0)

    def gather(pair, carry):
        rows, select, rest = [], [], []
        for side in range(2):
            source = 2 * pair + side
            aux = in_ref[source, TOK:QA].astype(F32)
            at = aux.astype(jnp.int32)
            later = later_ref[source]
            rest0 = jnp.sum(jnp.where(memory == at[1:2], later, 0.0), axis=0, keepdims=True)
            rest1 = jnp.sum(jnp.where(memory == at[3:4], later, 0.0), axis=0, keepdims=True)
            first, second = own_slots(aux, cap)
            hit0, hit1 = place == first, place == second
            select.append(spread(jnp.where(hit0 | hit1, 1.0, 0.0), cap, side).astype(BF16))
            own = jnp.where(hit0, rest0, jnp.where(hit1, rest1, 0.0))
            own = jnp.broadcast_to(jnp.sum(own, axis=1, keepdims=True), own.shape)
            rest.append(own.reshape(memories, cap, TOK))
            k, v = in_ref[source, QA : QA + TOK], in_ref[source, QA + TOK : QA + 2 * TOK]
            rows.append(jnp.concatenate([k, v], axis=1))
        rest = jnp.concatenate(rest, axis=1)
        got = dot(jnp.concatenate(select, axis=1), jnp.concatenate(rows, axis=0)).astype(BF16)
        at = pl.ds(pl.multiple_of(pair * 2 * cap, 2 * cap), 2 * cap)
        for m in range(memories):
            slots_ref[m, at, :] = got[m * 2 * cap : (m + 1) * 2 * cap]
            rest_ref[m, at, :] = rest[m]
        leaving(pair).start()
        return carry

    def leaving(pair):
        at = pl.ds(pl.multiple_of(pair * 2 * cap, 2 * cap), 2 * cap)
        return pltpu.make_async_copy(slots_ref.at[:, at], slots_out.at[:, at], slots_sem.at[pair])

    lax.fori_loop(0, sources // 2, gather, 0, unroll=2)

    row = iota((AUX, HD), 0)
    for m in range(memories):
        aux = jnp.zeros((AUX, HD), F32)
        for at, part in enumerate(three_parts(total[m : m + 1])):
            aux = jnp.where(row == at, part, aux)
        for half in range(2):
            update_ref[2 * m + half, PART_ROWS : PART_ROWS + AUX] = aux.astype(BF16)

    def updated(step):
        at = pl.ds(step * 8, 8)
        return pltpu.make_async_copy(update_ref.at[at], update_out.at[at], update_sem.at[step])

    def update(step, carry):
        for m in range(4):
            m = 4 * step + m
            k = slots_ref[m, :, 0:HD].astype(F32)
            v = slots_ref[m, :, HD : 2 * HD]
            kd = (k * jnp.exp(-rates_ref[pl.ds(m, 1), :] * rest_ref[m])).astype(BF16)
            added = tn(kd, v).astype(BF16)
            for half in range(2):
                part = added[half * PART_ROWS : (half + 1) * PART_ROWS]
                update_ref[2 * m + half, 0:PART_ROWS] = part
        updated(step).start()
        return carry

    lax.fori_loop(0, memories // 4, update, 0)
    for step in range(memories // 4):
        updated(step).wait()
    for pair in range(sources // 2):
        leaving(pair).wait()


def scan_kernel(in_ref, out_ref):
    state = jnp.zeros((PART_ROWS, HD), F32)
    for part in range(in_ref.shape[0]):
        out_ref[part] = state.astype(BF16)
        aux = in_ref[part, PART_ROWS : PART_ROWS + AUX].astype(F32)
        fade = jnp.exp(aux[0:1] + aux[1:2] + aux[2:3])
        state = fade * state + in_ref[part, 0:PART_ROWS].astype(F32)


def beside_kernel(
    cap,
    in_ref,
    kv_hbm,
    rate_ref,
    raw_hbm,
    rest_hbm,
    kv_ref,
    qg_ref,
    raw_ref,
    rest_ref,
    rates_ref,
    sums_ref,
    kv_sem,
    pick_sem,
    raw_sem,
    faded_sem,
):
    memories, slots, _ = kv_ref.shape
    pairs = in_ref.shape[0] // 2
    width = memories * 2 * cap
    each = width // slots

    def kv_in(step):
        four = pl.ds(4 * step, 4)
        return pltpu.make_async_copy(kv_hbm.at[four], kv_ref.at[four], kv_sem.at[step])

    def pick_out(pair):
        at = pl.ds(memories + each * pair, each)
        return pltpu.make_async_copy(rest_ref.at[at], rest_hbm.at[at], pick_sem.at[pair])

    def made_out(step):
        two = pl.ds(2 * step, 2)
        return (
            pltpu.make_async_copy(raw_ref.at[two], raw_hbm.at[two], raw_sem.at[step]),
            pltpu.make_async_copy(rest_ref.at[two], rest_hbm.at[two], faded_sem.at[step]),
        )

    for step in range(memories // 4):
        kv_in(step).start()
    head_rates(rate_ref, own_head(), rates_ref)
    tri = iota((TOK, TOK), 0) - iota((TOK, TOK), 1)
    sums_ref[0:TOK] = (tri >= 0).astype(BF16)
    sums_ref[TOK : 2 * TOK] = (tri < 0).astype(BF16)
    ones = jnp.ones((TOK, HD), BF16)
    eye = (tri == 0).astype(BF16)
    down, across = iota((width // 2, TOK), 0), iota((TOK, width), 1)

    def route(pair, carry):
        rows, select, pick = [], [], jnp.zeros((TOK, width), F32)
        for side in range(2):
            packed = in_ref[2 * pair + side, TOK:QA]
            aux = packed.astype(F32)
            gamma = dot(jnp.where(tri == 0, aux[0:1], 0.0).astype(BF16), ones).astype(BF16)
            rows.append(jnp.concatenate([in_ref[2 * pair + side, 0:TOK], gamma], axis=1))
            first, second = own_slots(aux, cap)
            hit = (down == first) | (down == second)
            select.append(spread(jnp.where(hit, 1.0, 0.0), cap, side).astype(BF16))
            aux = nt(eye, packed)
            at = aux.astype(jnp.int32)
            first = at[:, 1:2] * (2 * cap) + at[:, 2:3] + side * cap
            second = at[:, 3:4] * (2 * cap) + at[:, 4:5] + side * cap
            w0 = aux[:, 5:6] + aux[:, 7:8] + aux[:, 9:10]
            w1 = aux[:, 6:7] + aux[:, 8:9] + aux[:, 10:11]
            pick = jnp.where(across == first, w0, jnp.where(across == second, w1, pick))
        for square in range(width // TOK):
            which, row = divmod(square * TOK, slots)
            lanes = slice(square * TOK, (square + 1) * TOK)
            at = memories + each * pair + which
            rest_ref[at, row : row + TOK] = pick[:, lanes].astype(BF16)
        pick_out(pair).start()
        got = dot(jnp.concatenate(select, axis=1), jnp.concatenate(rows, axis=0)).astype(BF16)
        at = pl.ds(pl.multiple_of(pair * 2 * cap, 2 * cap), 2 * cap)
        for m in range(memories):
            qg_ref[m, at, :] = got[m * 2 * cap : (m + 1) * 2 * cap]
        return carry

    lax.fori_loop(0, pairs, route, 0)
    for step in range(memories // 4):
        kv_in(step).wait()

    def intra(step, carry):
        for m in (2 * step, 2 * step + 1):
            rate = rates_ref[pl.ds(m, 1), :]
            behind = []
            faded_all = jnp.ones((1, HD), F32)
            scores = nt(qg_ref[m, :, 0:HD], kv_ref[m, :, 0:HD])
            table = []
            for b in range(slots // TOK):
                at = slice(b * TOK, (b + 1) * TOK)
                seen = slice(0, (b + 1) * TOK)
                q = qg_ref[m, at, 0:HD]
                gamma = qg_ref[m, at, HD : 2 * HD]
                masked = jnp.where(tri > 0, gamma.astype(F32), 0.0).astype(BF16)
                sums = dot(sums_ref[...], jnp.concatenate([masked, gamma], axis=1))
                inside = jnp.where(tri >= 0, jnp.exp(-rate * sums[0:TOK, 0:TOK]), 0.0)
                fade = jnp.exp(-rate * sums[0:TOK, TOK : 2 * TOK])
                rest_ref[m, at] = (q.astype(F32) * (fade * faded_all)).astype(BF16)
                decay = jnp.concatenate([fade * row for row in behind] + [inside], axis=1)
                weights = (decay * scores[at, seen]).astype(BF16)
                if (b + 1) * TOK < slots:
                    zeros = jnp.zeros((TOK, slots - (b + 1) * TOK), BF16)
                    weights = jnp.concatenate([weights, zeros], axis=1)
                    whole = fade[TOK - 1 : TOK]
                    faded_all = faded_all * whole
                    rest = jnp.exp(-rate * sums[TOK : 2 * TOK, TOK : 2 * TOK])
                    behind = [row * whole for row in behind] + [rest.T]
                table.append(weights)
            raw_ref[m] = dot(jnp.concatenate(table, axis=0), kv_ref[m, :, HD : 2 * HD])
        for copy in made_out(step):
            copy.start()
        return carry

    lax.fori_loop(0, memories // 2, intra, 0, unroll=2)
    for pair in range(pairs):
        pick_out(pair).wait()
    for step in range(memories // 2):
        for copy in made_out(step):
            copy.wait()


def finish_kernel(cap, rest_ref, raw_ref, state_ref, gain_ref, out_ref, made_ref):
    memories, slots, _ = raw_ref.shape
    width = memories * 2 * cap
    each = width // slots
    even = iota((slots, HD), 0) % (2 * cap) < cap

    def one(m, carry):
        raw = raw_ref[m] + dot(rest_ref[m], state_ref[m])
        mean = jnp.mean(raw * raw, axis=1, keepdims=True)
        made = raw * lax.rsqrt(mean + EPS)
        made_ref[m, :, 0:HD] = jnp.where(even, made, 0.0).astype(BF16)
        made_ref[m, :, HD : 2 * HD] = jnp.where(even, 0.0, made).astype(BF16)
        return carry

    lax.fori_loop(0, memories, one, 0, unroll=8)
    gain = gain_ref[pl.ds(own_head(), 1), :]

    def mix(pair, carry):
        at = pl.ds(pl.multiple_of(pair * 2 * cap, 2 * cap), 2 * cap)
        rows = jnp.concatenate([made_ref[m, at, :] for m in range(memories)], axis=0)
        squares = []
        for square in range(width // TOK):
            which, row = divmod(square * TOK, slots)
            squares.append(rest_ref[memories + each * pair + which, row : row + TOK])
        mixed = dot(jnp.concatenate(squares, axis=1), rows)
        for side in range(2):
            own = mixed[:, side * HD : (side + 1) * HD]
            out_ref[2 * pair + side] = (gain * own).astype(BF16)
        return carry

    lax.fori_loop(0, out_ref.shape[0] // 2, mix, 0, unroll=8)


def unpack_kernel(in_ref, out_ref):
    for h in range(in_ref.shape[0]):
        out_ref[:, h * HD : (h + 1) * HD] = in_ref[h]


like = jax.ShapeDtypeStruct
ANY = pl.BlockSpec(memory_space=pl.ANY)
WHOLE = pl.BlockSpec(memory_space=pltpu.VMEM)
DMA = pltpu.SemaphoreType.DMA


def call(kernel, outs, ins, out_specs, room, scratch=(), grid=(), flops=0, moved=0):
    return pl.pallas_call(
        kernel,
        out_shape=outs,
        grid=grid,
        in_specs=ins,
        out_specs=out_specs,
        scratch_shapes=list(scratch),
        compiler_params=pltpu.CompilerParams(vmem_limit_bytes=VMEM_ALL - room),
        cost_estimate=pl.CostEstimate(flops=flops, bytes_accessed=moved, transcendentals=0),
    )


def pack(heads):
    return call(
        lambda *refs: pack_kernel(heads, *refs),
        like((heads, QA + 2 * TOK, HD), BF16),
        [ANY] * 6,
        ANY,
        -2_000_000,
        (
            pltpu.VMEM((heads, TOK), BF16),
            pltpu.VMEM((2, TOK), jnp.int32),
            pltpu.VMEM((2, TOK), F32),
            pltpu.VMEM((3, TOK, heads * HD), BF16),
            pltpu.VMEM((heads, QA + 2 * TOK, HD), BF16),
            DMA((3,)),
            DMA((3, GROUPS)),
            DMA((GROUPS,)),
        ),
    )


def gather(memories, sources, parts):
    cap = 3 * TOK // memories
    slots = sources * cap
    return call(
        lambda *refs: gather_kernel(cap, *refs),
        (
            like((memories, slots, 2 * HD), BF16),
            like((parts, PART_ROWS + AUX, HD), BF16),
        ),
        [WHOLE, WHOLE],
        (ANY, ANY),
        ROOM,
        (
            pltpu.VMEM((memories, slots, 2 * HD), BF16),
            pltpu.VMEM((memories, slots, HD), F32),
            pltpu.VMEM((parts, PART_ROWS + AUX, HD), BF16),
            pltpu.VMEM((memories, HD), F32),
            pltpu.VMEM((sources, memories, TOK), F32),
            DMA((sources // 2,)),
            DMA((memories // 4,)),
        ),
    )


def scan(parts):
    return call(
        scan_kernel,
        like((parts, PART_ROWS, HD), BF16),
        [WHOLE],
        WHOLE,
        40_000_000,
        flops=2 * 10**10,
        moved=2**20,
    )


def beside(memories, sources):
    cap = 3 * TOK // memories
    slots = sources * cap
    pairs = sources // 2
    rest = (memories + pairs * memories * 2 * cap // slots, slots, HD)
    return call(
        lambda *refs: beside_kernel(cap, *refs),
        (like((memories, slots, HD), F32), like(rest, BF16)),
        [WHOLE, ANY, WHOLE],
        (ANY, ANY),
        ROOM,
        (
            pltpu.VMEM((memories, slots, 2 * HD), BF16),
            pltpu.VMEM((memories, slots, 2 * HD), BF16),
            pltpu.VMEM((memories, slots, HD), F32),
            pltpu.VMEM(rest, BF16),
            pltpu.VMEM((memories, HD), F32),
            pltpu.VMEM((2 * TOK, TOK), BF16),
            DMA((memories // 4,)),
            DMA((pairs,)),
            DMA((memories // 2,)),
            DMA((memories // 2,)),
        ),
        flops=15 * 10**9,
        moved=12 * 2**20,
    )


def finish(memories, sources):
    cap = 3 * TOK // memories
    slots = sources * cap
    return call(
        lambda *refs: finish_kernel(cap, *refs),
        like((sources, TOK, HD), BF16),
        [WHOLE] * 4,
        WHOLE,
        40_000_000,
        (pltpu.VMEM((memories, slots, 2 * HD), BF16),),
    )


def unpack(heads):
    return call(unpack_kernel, like((TOK, heads * HD), BF16), [WHOLE], WHOLE, 40_000_000)


def body(queries, keys, values, gamma, rate, route_ids, route_weights, norm_gain):
    heads = gamma.shape[1]
    memories = rate.shape[0]
    sources = lax.axis_size("mem")
    parts = lax.axis_size("seq")
    send = pack(heads)(queries, keys, values, gamma.T, route_ids.T, route_weights.T)
    arrived = lax.all_to_all(send, "mem", 0, 0, tiled=True)
    slot_rows, update = gather(memories, sources, parts)(arrived, rate)
    pieces = lax.all_to_all(update, "seq", 0, 0, tiled=True)
    raw, rest = beside(memories, sources)(arrived, slot_rows, rate)
    pieces, raw, rest = lax.optimization_barrier((pieces, raw, rest))
    before = scan(parts)(pieces)
    state = lax.all_to_all(before, "seq", 0, 0, tiled=True).reshape(memories, HD, HD)
    gain = norm_gain.reshape(heads, HD)
    mixed = finish(memories, sources)(rest, raw, state, gain)
    returned = lax.all_to_all(mixed, "mem", 0, 0, tiled=True)
    return unpack(heads)(returned)


def solution(mesh):
    split = P(("seq", "mem"), None)
    return jax.shard_map(
        body,
        mesh=mesh,
        in_specs=(split, split, split, split, P(), split, split, P()),
        out_specs=split,
        check_vma=False,
    )
```

```python
import jax
import jax.numpy as jnp
from jax import lax
from jax.experimental import pallas as pl
from jax.experimental.pallas import tpu as pltpu
from jax.sharding import PartitionSpec as P

F32, BF16 = jnp.float32, jnp.bfloat16
TOK = 128
HD = 128
AUX = 16
QA = TOK + AUX
PART_ROWS = 64
GROUPS = 2
EPS = 1e-6
VMEM_ALL = 58_000_000
ROOM = 4_200_000


def iota(shape, dim):
    return lax.broadcasted_iota(jnp.int32, shape, dim)


def nt(a, b):
    return lax.dot_general(a, b, (((1,), (1,)), ((), ())), preferred_element_type=F32)


def tn(a, b):
    return lax.dot_general(a, b, (((0,), (0,)), ((), ())), preferred_element_type=F32)


def dot(a, b):
    return jnp.dot(a, b, preferred_element_type=F32)


def three_parts(x):
    hi = x.astype(BF16).astype(F32)
    mid = (x - hi).astype(BF16).astype(F32)
    return hi, mid, x - hi - mid


def own_head():
    return lax.axis_index("mem")


def pack_kernel(
    heads, q_ref, k_ref, v_ref, gamma_hbm, ids_hbm, weights_hbm, out_ref, gamma_ref, ids_ref, weights_ref, given_ref, rows_ref, small_sem, sem, out_sem
):
    groups, lanes = out_sem.shape[0], heads * HD // out_sem.shape[0]

    def arriving(group):
        at = slice(group * lanes, (group + 1) * lanes)
        return [
            pltpu.make_async_copy(ref.at[:, at], given_ref.at[which, :, at], sem.at[which, group])
            for which, ref in enumerate((q_ref, k_ref, v_ref))
        ]

    small = [
        pltpu.make_async_copy(gamma_hbm, gamma_ref, small_sem.at[0]),
        pltpu.make_async_copy(ids_hbm, ids_ref, small_sem.at[1]),
        pltpu.make_async_copy(weights_hbm, weights_ref, small_sem.at[2]),
    ]
    for copy in small:
        copy.start()
    for group in range(groups):
        for copy in arriving(group):
            copy.start()
    for copy in small:
        copy.wait()
    ids = ids_ref[...]
    w_hi, w_mid, w_lo = three_parts(weights_ref[...])
    memory = iota((heads, TOK), 0)
    hit0, hit1 = memory == ids[0:1], memory == ids[1:2]
    hits = jnp.where(hit0 | hit1, 1.0, 0.0).astype(BF16)
    earlier = (iota((TOK, TOK), 0) < iota((TOK, TOK), 1)).astype(BF16)
    before = dot(hits, earlier)
    rank0 = jnp.sum(jnp.where(hit0, before, 0.0), axis=0, keepdims=True)
    rank1 = jnp.sum(jnp.where(hit1, before, 0.0), axis=0, keepdims=True)
    row = iota((AUX, TOK), 0)
    shared = jnp.zeros((AUX, TOK), F32)
    entries = [ids[0:1].astype(F32), rank0, ids[1:2].astype(F32), rank1]
    for part in (w_hi, w_mid, w_lo):
        entries += [part[0:1], part[1:2]]
    for at, entry in enumerate(entries):
        shared = jnp.where(row == at + 1, entry, shared)
    gamma_rows = gamma_ref[...].astype(F32)
    for h in range(heads):
        aux = jnp.where(row == 0, gamma_rows[h : h + 1], shared)
        rows_ref[h, TOK:QA] = aux.astype(BF16)
    leaving = []
    for group in range(groups):
        for copy in arriving(group):
            copy.wait()
        some = range(group * heads // groups, (group + 1) * heads // groups)
        for h in some:
            for which, at in enumerate((0, QA, QA + TOK)):
                rows_ref[h, at : at + TOK] = given_ref[which, :, h * HD : (h + 1) * HD]
        at = pl.ds(some[0], len(some))
        leaving.append(pltpu.make_async_copy(rows_ref.at[at], out_ref.at[at], out_sem.at[group]))
        leaving[group].start()
    for copy in leaving:
        copy.wait()


def head_rates(rate_ref, head, scratch_ref):
    rates = rate_ref[...].astype(F32)
    mine = jnp.where(iota(rates.shape, 1) == head, rates, 0.0)
    scratch_ref[...] = jnp.broadcast_to(jnp.sum(mine, axis=1, keepdims=True), scratch_ref.shape)


def own_slots(aux, cap):
    at = aux[0:8].astype(jnp.int32)
    return at[1:2] * cap + at[2:3], at[3:4] * cap + at[4:5]


def spread(rows, cap, side):
    parts = rows.reshape(-1, cap, rows.shape[1])
    parts = [parts, jnp.zeros_like(parts)][:: 1 - 2 * side]
    return jnp.concatenate(parts, axis=1).reshape(-1, rows.shape[1])


def gather_kernel(
    cap, in_ref, rate_ref, slots_out, update_out, slots_ref, rest_ref, update_ref, rates_ref, later_ref, slots_sem, update_sem
):
    sources = in_ref.shape[0]
    memories, slots, _ = slots_ref.shape
    width = memories * 2 * cap

    head_rates(rate_ref, own_head(), rates_ref)
    after = (iota((TOK, TOK), 0) > iota((TOK, TOK), 1)).astype(BF16)
    memory = iota((memories, TOK), 0)
    hits, gammas = [], []
    for source in range(sources):
        aux = in_ref[source, TOK:QA].astype(F32)
        at = aux.astype(jnp.int32)
        hit = (memory == at[1:2]) | (memory == at[3:4])
        gammas.append(jnp.where(hit, aux[0:1], 0.0))
    inside = dot(jnp.concatenate(gammas, axis=0).astype(BF16), after)
    behind = jnp.zeros((memories, 1), F32)
    for source in reversed(range(sources)):
        own = inside[source * memories : (source + 1) * memories]
        later_ref[source] = own + behind
        behind = behind + own[:, 0:1] + gammas[source][:, 0:1]
    total = -rates_ref[...] * behind

    place = iota((width // 2, TOK), 0)

    def gather(pair, carry):
        rows, select, rest = [], [], []
        for side in range(2):
            source = 2 * pair + side
            aux = in_ref[source, TOK:QA].astype(F32)
            at = aux.astype(jnp.int32)
            later = later_ref[source]
            rest0 = jnp.sum(jnp.where(memory == at[1:2], later, 0.0), axis=0, keepdims=True)
            rest1 = jnp.sum(jnp.where(memory == at[3:4], later, 0.0), axis=0, keepdims=True)
            first, second = own_slots(aux, cap)
            hit0, hit1 = place == first, place == second
            select.append(spread(jnp.where(hit0 | hit1, 1.0, 0.0), cap, side).astype(BF16))
            own = jnp.where(hit0, rest0, jnp.where(hit1, rest1, 0.0))
            own = jnp.broadcast_to(jnp.sum(own, axis=1, keepdims=True), own.shape)
            rest.append(own.reshape(memories, cap, TOK))
            k, v = in_ref[source, QA : QA + TOK], in_ref[source, QA + TOK : QA + 2 * TOK]
            rows.append(jnp.concatenate([k, v], axis=1))
        rest = jnp.concatenate(rest, axis=1)
        got = dot(jnp.concatenate(select, axis=1), jnp.concatenate(rows, axis=0)).astype(BF16)
        at = pl.ds(pl.multiple_of(pair * 2 * cap, 2 * cap), 2 * cap)
        for m in range(memories):
            slots_ref[m, at, :] = got[m * 2 * cap : (m + 1) * 2 * cap]
            rest_ref[m, at, :] = rest[m]
        leaving(pair).start()
        return carry

    def leaving(pair):
        at = pl.ds(pl.multiple_of(pair * 2 * cap, 2 * cap), 2 * cap)
        return pltpu.make_async_copy(slots_ref.at[:, at], slots_out.at[:, at], slots_sem.at[pair])

    lax.fori_loop(0, sources // 2, gather, 0, unroll=4)

    row = iota((AUX, HD), 0)
    for m in range(memories):
        aux = jnp.zeros((AUX, HD), F32)
        for at, part in enumerate(three_parts(total[m : m + 1])):
            aux = jnp.where(row == at, part, aux)
        for half in range(2):
            update_ref[2 * m + half, PART_ROWS : PART_ROWS + AUX] = aux.astype(BF16)

    def updated(step):
        at = pl.ds(step * 8, 8)
        return pltpu.make_async_copy(update_ref.at[at], update_out.at[at], update_sem.at[step])

    def update(step, carry):
        for m in range(4):
            m = 4 * step + m
            k = slots_ref[m, :, 0:HD].astype(F32)
            v = slots_ref[m, :, HD : 2 * HD]
            kd = (k * jnp.exp(-rates_ref[pl.ds(m, 1), :] * rest_ref[m])).astype(BF16)
            added = tn(kd, v).astype(BF16)
            for half in range(2):
                part = added[half * PART_ROWS : (half + 1) * PART_ROWS]
                update_ref[2 * m + half, 0:PART_ROWS] = part
        updated(step).start()
        return carry

    lax.fori_loop(0, memories // 4, update, 0, unroll=4)
    for step in range(memories // 4):
        updated(step).wait()
    for pair in range(sources // 2):
        leaving(pair).wait()


def scan_kernel(in_ref, out_ref):
    state = jnp.zeros((PART_ROWS, HD), F32)
    for part in range(in_ref.shape[0]):
        out_ref[part] = state.astype(BF16)
        aux = in_ref[part, PART_ROWS : PART_ROWS + AUX].astype(F32)
        fade = jnp.exp(aux[0:1] + aux[1:2] + aux[2:3])
        state = fade * state + in_ref[part, 0:PART_ROWS].astype(F32)


def beside_kernel(
    cap,
    in_ref,
    kv_hbm,
    rate_ref,
    raw_hbm,
    rest_hbm,
    kv_ref,
    qg_ref,
    raw_ref,
    rest_ref,
    rates_ref,
    sums_ref,
    kv_sem,
    pick_sem,
    raw_sem,
    faded_sem,
):
    memories, slots, _ = kv_ref.shape
    pairs = in_ref.shape[0] // 2
    width = memories * 2 * cap
    each = width // slots

    def kv_in(step):
        four = pl.ds(4 * step, 4)
        return pltpu.make_async_copy(kv_hbm.at[four], kv_ref.at[four], kv_sem.at[step])

    def pick_out(pair):
        at = pl.ds(memories + each * pair, each)
        return pltpu.make_async_copy(rest_ref.at[at], rest_hbm.at[at], pick_sem.at[pair])

    def made_out(step):
        two = pl.ds(2 * step, 2)
        return (
            pltpu.make_async_copy(raw_ref.at[two], raw_hbm.at[two], raw_sem.at[step]),
            pltpu.make_async_copy(rest_ref.at[two], rest_hbm.at[two], faded_sem.at[step]),
        )

    for step in range(memories // 4):
        kv_in(step).start()
    head_rates(rate_ref, own_head(), rates_ref)
    tri = iota((TOK, TOK), 0) - iota((TOK, TOK), 1)
    sums_ref[0:TOK] = (tri >= 0).astype(BF16)
    sums_ref[TOK : 2 * TOK] = (tri < 0).astype(BF16)
    ones = jnp.ones((TOK, HD), BF16)
    eye = (tri == 0).astype(BF16)
    down, across = iota((width // 2, TOK), 0), iota((TOK, width), 1)

    def route(pair, carry):
        rows, select, pick = [], [], jnp.zeros((TOK, width), F32)
        for side in range(2):
            packed = in_ref[2 * pair + side, TOK:QA]
            aux = packed.astype(F32)
            gamma = dot(jnp.where(tri == 0, aux[0:1], 0.0).astype(BF16), ones).astype(BF16)
            rows.append(jnp.concatenate([in_ref[2 * pair + side, 0:TOK], gamma], axis=1))
            first, second = own_slots(aux, cap)
            hit = (down == first) | (down == second)
            select.append(spread(jnp.where(hit, 1.0, 0.0), cap, side).astype(BF16))
            aux = nt(eye, packed)
            at = aux.astype(jnp.int32)
            first = at[:, 1:2] * (2 * cap) + at[:, 2:3] + side * cap
            second = at[:, 3:4] * (2 * cap) + at[:, 4:5] + side * cap
            w0 = aux[:, 5:6] + aux[:, 7:8] + aux[:, 9:10]
            w1 = aux[:, 6:7] + aux[:, 8:9] + aux[:, 10:11]
            pick = jnp.where(across == first, w0, jnp.where(across == second, w1, pick))
        for square in range(width // TOK):
            which, row = divmod(square * TOK, slots)
            lanes = slice(square * TOK, (square + 1) * TOK)
            at = memories + each * pair + which
            rest_ref[at, row : row + TOK] = pick[:, lanes].astype(BF16)
        pick_out(pair).start()
        got = dot(jnp.concatenate(select, axis=1), jnp.concatenate(rows, axis=0)).astype(BF16)
        at = pl.ds(pl.multiple_of(pair * 2 * cap, 2 * cap), 2 * cap)
        for m in range(memories):
            qg_ref[m, at, :] = got[m * 2 * cap : (m + 1) * 2 * cap]
        return carry

    lax.fori_loop(0, pairs, route, 0)
    for step in range(memories // 4):
        kv_in(step).wait()

    def intra(step, carry):
        for m in (2 * step, 2 * step + 1):
            rate = rates_ref[pl.ds(m, 1), :]
            behind = []
            faded_all = jnp.ones((1, HD), F32)
            scores = nt(qg_ref[m, :, 0:HD], kv_ref[m, :, 0:HD])
            table = []
            for b in range(slots // TOK):
                at = slice(b * TOK, (b + 1) * TOK)
                seen = slice(0, (b + 1) * TOK)
                q = qg_ref[m, at, 0:HD]
                gamma = qg_ref[m, at, HD : 2 * HD]
                masked = jnp.where(tri > 0, gamma.astype(F32), 0.0).astype(BF16)
                sums = dot(sums_ref[...], jnp.concatenate([masked, gamma], axis=1))
                inside = jnp.where(tri >= 0, jnp.exp(-rate * sums[0:TOK, 0:TOK]), 0.0)
                fade = jnp.exp(-rate * sums[0:TOK, TOK : 2 * TOK])
                rest_ref[m, at] = (q.astype(F32) * (fade * faded_all)).astype(BF16)
                decay = jnp.concatenate([fade * row for row in behind] + [inside], axis=1)
                weights = (decay * scores[at, seen]).astype(BF16)
                if (b + 1) * TOK < slots:
                    zeros = jnp.zeros((TOK, slots - (b + 1) * TOK), BF16)
                    weights = jnp.concatenate([weights, zeros], axis=1)
                    whole = fade[TOK - 1 : TOK]
                    faded_all = faded_all * whole
                    rest = jnp.exp(-rate * sums[TOK : 2 * TOK, TOK : 2 * TOK])
                    behind = [row * whole for row in behind] + [rest.T]
                table.append(weights)
            raw_ref[m] = dot(jnp.concatenate(table, axis=0), kv_ref[m, :, HD : 2 * HD])
        for copy in made_out(step):
            copy.start()
        return carry

    lax.fori_loop(0, memories // 2, intra, 0, unroll=2)
    for pair in range(pairs):
        pick_out(pair).wait()
    for step in range(memories // 2):
        for copy in made_out(step):
            copy.wait()


def finish_kernel(cap, rest_ref, raw_ref, state_ref, gain_ref, out_ref, made_ref):
    memories, slots, _ = raw_ref.shape
    width = memories * 2 * cap
    each = width // slots
    even = iota((slots, HD), 0) % (2 * cap) < cap

    def one(m, carry):
        raw = raw_ref[m] + dot(rest_ref[m], state_ref[m])
        mean = jnp.mean(raw * raw, axis=1, keepdims=True)
        made = raw * lax.rsqrt(mean + EPS)
        made_ref[m, :, 0:HD] = jnp.where(even, made, 0.0).astype(BF16)
        made_ref[m, :, HD : 2 * HD] = jnp.where(even, 0.0, made).astype(BF16)
        return carry

    lax.fori_loop(0, memories, one, 0, unroll=16)
    gain = gain_ref[pl.ds(own_head(), 1), :]

    def mix(pair, carry):
        at = pl.ds(pl.multiple_of(pair * 2 * cap, 2 * cap), 2 * cap)
        rows = jnp.concatenate([made_ref[m, at, :] for m in range(memories)], axis=0)
        squares = []
        for square in range(width // TOK):
            which, row = divmod(square * TOK, slots)
            squares.append(rest_ref[memories + each * pair + which, row : row + TOK])
        mixed = dot(jnp.concatenate(squares, axis=1), rows)
        for side in range(2):
            own = mixed[:, side * HD : (side + 1) * HD]
            out_ref[2 * pair + side] = (gain * own).astype(BF16)
        return carry

    lax.fori_loop(0, out_ref.shape[0] // 2, mix, 0, unroll=8)


def unpack_kernel(in_ref, out_ref):
    for h in range(in_ref.shape[0]):
        out_ref[:, h * HD : (h + 1) * HD] = in_ref[h]


like = jax.ShapeDtypeStruct
ANY = pl.BlockSpec(memory_space=pl.ANY)
WHOLE = pl.BlockSpec(memory_space=pltpu.VMEM)
DMA = pltpu.SemaphoreType.DMA


def call(kernel, outs, ins, out_specs, room, scratch=(), grid=(), flops=0, moved=0):
    return pl.pallas_call(
        kernel,
        out_shape=outs,
        grid=grid,
        in_specs=ins,
        out_specs=out_specs,
        scratch_shapes=list(scratch),
        compiler_params=pltpu.CompilerParams(vmem_limit_bytes=VMEM_ALL - room),
        cost_estimate=pl.CostEstimate(flops=flops, bytes_accessed=moved, transcendentals=0),
    )


def pack(heads):
    return call(
        lambda *refs: pack_kernel(heads, *refs),
        like((heads, QA + 2 * TOK, HD), BF16),
        [ANY] * 6,
        ANY,
        -2_000_000,
        (
            pltpu.VMEM((heads, TOK), BF16),
            pltpu.VMEM((2, TOK), jnp.int32),
            pltpu.VMEM((2, TOK), F32),
            pltpu.VMEM((3, TOK, heads * HD), BF16),
            pltpu.VMEM((heads, QA + 2 * TOK, HD), BF16),
            DMA((3,)),
            DMA((3, GROUPS)),
            DMA((GROUPS,)),
        ),
    )


def gather(memories, sources, parts):
    cap = 3 * TOK // memories
    slots = sources * cap
    return call(
        lambda *refs: gather_kernel(cap, *refs),
        (
            like((memories, slots, 2 * HD), BF16),
            like((parts, PART_ROWS + AUX, HD), BF16),
        ),
        [WHOLE, WHOLE],
        (ANY, ANY),
        ROOM,
        (
            pltpu.VMEM((memories, slots, 2 * HD), BF16),
            pltpu.VMEM((memories, slots, HD), F32),
            pltpu.VMEM((parts, PART_ROWS + AUX, HD), BF16),
            pltpu.VMEM((memories, HD), F32),
            pltpu.VMEM((sources, memories, TOK), F32),
            DMA((sources // 2,)),
            DMA((memories // 4,)),
        ),
    )


def scan(parts):
    return call(
        scan_kernel,
        like((parts, PART_ROWS, HD), BF16),
        [WHOLE],
        WHOLE,
        40_000_000,
        flops=2 * 10**10,
        moved=2**20,
    )


def beside(memories, sources):
    cap = 3 * TOK // memories
    slots = sources * cap
    pairs = sources // 2
    rest = (memories + pairs * memories * 2 * cap // slots, slots, HD)
    return call(
        lambda *refs: beside_kernel(cap, *refs),
        (like((memories, slots, HD), F32), like(rest, BF16)),
        [WHOLE, ANY, WHOLE],
        (ANY, ANY),
        ROOM,
        (
            pltpu.VMEM((memories, slots, 2 * HD), BF16),
            pltpu.VMEM((memories, slots, 2 * HD), BF16),
            pltpu.VMEM((memories, slots, HD), F32),
            pltpu.VMEM(rest, BF16),
            pltpu.VMEM((memories, HD), F32),
            pltpu.VMEM((2 * TOK, TOK), BF16),
            DMA((memories // 4,)),
            DMA((pairs,)),
            DMA((memories // 2,)),
            DMA((memories // 2,)),
        ),
        flops=15 * 10**9,
        moved=12 * 2**20,
    )


def finish(memories, sources):
    cap = 3 * TOK // memories
    slots = sources * cap
    return call(
        lambda *refs: finish_kernel(cap, *refs),
        like((sources, TOK, HD), BF16),
        [WHOLE] * 4,
        WHOLE,
        40_000_000,
        (pltpu.VMEM((memories, slots, 2 * HD), BF16),),
    )


def unpack(heads):
    return call(unpack_kernel, like((TOK, heads * HD), BF16), [WHOLE], WHOLE, 40_000_000)


def body(queries, keys, values, gamma, rate, route_ids, route_weights, norm_gain):
    heads = gamma.shape[1]
    memories = rate.shape[0]
    sources = lax.axis_size("mem")
    parts = lax.axis_size("seq")
    send = pack(heads)(queries, keys, values, gamma.T, route_ids.T, route_weights.T)
    arrived = lax.all_to_all(send, "mem", 0, 0, tiled=True)
    slot_rows, update = gather(memories, sources, parts)(arrived, rate)
    pieces = lax.all_to_all(update, "seq", 0, 0, tiled=True)
    raw, rest = beside(memories, sources)(arrived, slot_rows, rate)
    pieces, raw, rest = lax.optimization_barrier((pieces, raw, rest))
    before = scan(parts)(pieces)
    state = lax.all_to_all(before, "seq", 0, 0, tiled=True).reshape(memories, HD, HD)
    gain = norm_gain.reshape(heads, HD)
    mixed = finish(memories, sources)(rest, raw, state, gain)
    returned = lax.all_to_all(mixed, "mem", 0, 0, tiled=True)
    return unpack(heads)(returned)


def solution(mesh):
    split = P(("seq", "mem"), None)
    return jax.shard_map(
        body,
        mesh=mesh,
        in_specs=(split, split, split, split, P(), split, split, P()),
        out_specs=split,
        check_vma=False,
    )
```

```python
import jax
import jax.numpy as jnp
from jax import lax
from jax.experimental import pallas as pl
from jax.experimental.pallas import tpu as pltpu
from jax.sharding import PartitionSpec as P

F32, BF16 = jnp.float32, jnp.bfloat16
TOK = 128
HD = 128
AUX = 16
QA = TOK + AUX
PART_ROWS = 64
GROUPS = 2
EPS = 1e-6
VMEM_ALL = 58_000_000
ROOM = 4_200_000


def iota(shape, dim):
    return lax.broadcasted_iota(jnp.int32, shape, dim)


def nt(a, b):
    return lax.dot_general(a, b, (((1,), (1,)), ((), ())), preferred_element_type=F32)


def tn(a, b):
    return lax.dot_general(a, b, (((0,), (0,)), ((), ())), preferred_element_type=F32)


def dot(a, b):
    return jnp.dot(a, b, preferred_element_type=F32)


def three_parts(x):
    hi = x.astype(BF16).astype(F32)
    mid = (x - hi).astype(BF16).astype(F32)
    return hi, mid, x - hi - mid


def own_head():
    return lax.axis_index("mem")


def pack_kernel(
    heads, q_ref, k_ref, v_ref, gamma_hbm, ids_hbm, weights_hbm, out_ref, gamma_ref, ids_ref, weights_ref, given_ref, rows_ref, small_sem, sem, out_sem
):
    groups, lanes = out_sem.shape[0], heads * HD // out_sem.shape[0]

    def arriving(group):
        at = slice(group * lanes, (group + 1) * lanes)
        return [
            pltpu.make_async_copy(ref.at[:, at], given_ref.at[which, :, at], sem.at[which, group])
            for which, ref in enumerate((q_ref, k_ref, v_ref))
        ]

    small = [
        pltpu.make_async_copy(gamma_hbm, gamma_ref, small_sem.at[0]),
        pltpu.make_async_copy(ids_hbm, ids_ref, small_sem.at[1]),
        pltpu.make_async_copy(weights_hbm, weights_ref, small_sem.at[2]),
    ]
    for copy in small:
        copy.start()
    for group in range(groups):
        for copy in arriving(group):
            copy.start()
    for copy in small:
        copy.wait()
    ids = ids_ref[...]
    w_hi, w_mid, w_lo = three_parts(weights_ref[...])
    memory = iota((heads, TOK), 0)
    hit0, hit1 = memory == ids[0:1], memory == ids[1:2]
    hits = jnp.where(hit0 | hit1, 1.0, 0.0).astype(BF16)
    earlier = (iota((TOK, TOK), 0) < iota((TOK, TOK), 1)).astype(BF16)
    before = dot(hits, earlier)
    rank0 = jnp.sum(jnp.where(hit0, before, 0.0), axis=0, keepdims=True)
    rank1 = jnp.sum(jnp.where(hit1, before, 0.0), axis=0, keepdims=True)
    row = iota((AUX, TOK), 0)
    shared = jnp.zeros((AUX, TOK), F32)
    entries = [ids[0:1].astype(F32), rank0, ids[1:2].astype(F32), rank1]
    for part in (w_hi, w_mid, w_lo):
        entries += [part[0:1], part[1:2]]
    for at, entry in enumerate(entries):
        shared = jnp.where(row == at + 1, entry, shared)
    gamma_rows = gamma_ref[...].astype(F32)
    for h in range(heads):
        aux = jnp.where(row == 0, gamma_rows[h : h + 1], shared)
        rows_ref[h, TOK:QA] = aux.astype(BF16)
    leaving = []
    for group in range(groups):
        for copy in arriving(group):
            copy.wait()
        some = range(group * heads // groups, (group + 1) * heads // groups)
        for h in some:
            for which, at in enumerate((0, QA, QA + TOK)):
                rows_ref[h, at : at + TOK] = given_ref[which, :, h * HD : (h + 1) * HD]
        at = pl.ds(some[0], len(some))
        leaving.append(pltpu.make_async_copy(rows_ref.at[at], out_ref.at[at], out_sem.at[group]))
        leaving[group].start()
    for copy in leaving:
        copy.wait()


def head_rates(rate_ref, head, scratch_ref):
    rates = rate_ref[...].astype(F32)
    mine = jnp.where(iota(rates.shape, 1) == head, rates, 0.0)
    scratch_ref[...] = jnp.broadcast_to(jnp.sum(mine, axis=1, keepdims=True), scratch_ref.shape)


def own_slots(aux, cap):
    at = aux[0:8].astype(jnp.int32)
    return at[1:2] * cap + at[2:3], at[3:4] * cap + at[4:5]


def spread(rows, cap, side):
    parts = rows.reshape(-1, cap, rows.shape[1])
    parts = [parts, jnp.zeros_like(parts)][:: 1 - 2 * side]
    return jnp.concatenate(parts, axis=1).reshape(-1, rows.shape[1])


def gather_kernel(
    cap, in_ref, rate_ref, slots_out, update_out, slots_ref, rest_ref, update_ref, rates_ref, later_ref, slots_sem, update_sem
):
    sources = in_ref.shape[0]
    memories, slots, _ = slots_ref.shape
    width = memories * 2 * cap

    head_rates(rate_ref, own_head(), rates_ref)
    after = (iota((TOK, TOK), 0) > iota((TOK, TOK), 1)).astype(BF16)
    memory = iota((memories, TOK), 0)
    hits, gammas = [], []
    for source in range(sources):
        aux = in_ref[source, TOK:QA].astype(F32)
        at = aux.astype(jnp.int32)
        hit = (memory == at[1:2]) | (memory == at[3:4])
        gammas.append(jnp.where(hit, aux[0:1], 0.0))
    inside = dot(jnp.concatenate(gammas, axis=0).astype(BF16), after)
    behind = jnp.zeros((memories, 1), F32)
    for source in reversed(range(sources)):
        own = inside[source * memories : (source + 1) * memories]
        later_ref[source] = own + behind
        behind = behind + own[:, 0:1] + gammas[source][:, 0:1]
    total = -rates_ref[...] * behind

    place = iota((width // 2, TOK), 0)

    def gather(pair, carry):
        rows, select, rest = [], [], []
        for side in range(2):
            source = 2 * pair + side
            aux = in_ref[source, TOK:QA].astype(F32)
            at = aux.astype(jnp.int32)
            later = later_ref[source]
            rest0 = jnp.sum(jnp.where(memory == at[1:2], later, 0.0), axis=0, keepdims=True)
            rest1 = jnp.sum(jnp.where(memory == at[3:4], later, 0.0), axis=0, keepdims=True)
            first, second = own_slots(aux, cap)
            hit0, hit1 = place == first, place == second
            select.append(spread(jnp.where(hit0 | hit1, 1.0, 0.0), cap, side).astype(BF16))
            own = jnp.where(hit0, rest0, jnp.where(hit1, rest1, 0.0))
            own = jnp.broadcast_to(jnp.sum(own, axis=1, keepdims=True), own.shape)
            rest.append(own.reshape(memories, cap, TOK))
            k, v = in_ref[source, QA : QA + TOK], in_ref[source, QA + TOK : QA + 2 * TOK]
            rows.append(jnp.concatenate([k, v], axis=1))
        rest = jnp.concatenate(rest, axis=1)
        got = dot(jnp.concatenate(select, axis=1), jnp.concatenate(rows, axis=0)).astype(BF16)
        at = pl.ds(pl.multiple_of(pair * 2 * cap, 2 * cap), 2 * cap)
        for m in range(memories):
            slots_ref[m, at, :] = got[m * 2 * cap : (m + 1) * 2 * cap]
            rest_ref[m, at, :] = rest[m]
        leaving(pair).start()
        return carry

    def leaving(pair):
        at = pl.ds(pl.multiple_of(pair * 2 * cap, 2 * cap), 2 * cap)
        return pltpu.make_async_copy(slots_ref.at[:, at], slots_out.at[:, at], slots_sem.at[pair])

    lax.fori_loop(0, sources // 2, gather, 0, unroll=8)

    row = iota((AUX, HD), 0)
    for m in range(memories):
        aux = jnp.zeros((AUX, HD), F32)
        for at, part in enumerate(three_parts(total[m : m + 1])):
            aux = jnp.where(row == at, part, aux)
        for half in range(2):
            update_ref[2 * m + half, PART_ROWS : PART_ROWS + AUX] = aux.astype(BF16)

    def updated(step):
        at = pl.ds(step * 8, 8)
        return pltpu.make_async_copy(update_ref.at[at], update_out.at[at], update_sem.at[step])

    def update(step, carry):
        for m in range(4):
            m = 4 * step + m
            k = slots_ref[m, :, 0:HD].astype(F32)
            v = slots_ref[m, :, HD : 2 * HD]
            kd = (k * jnp.exp(-rates_ref[pl.ds(m, 1), :] * rest_ref[m])).astype(BF16)
            added = tn(kd, v).astype(BF16)
            for half in range(2):
                part = added[half * PART_ROWS : (half + 1) * PART_ROWS]
                update_ref[2 * m + half, 0:PART_ROWS] = part
        updated(step).start()
        return carry

    lax.fori_loop(0, memories // 4, update, 0, unroll=4)
    for step in range(memories // 4):
        updated(step).wait()
    for pair in range(sources // 2):
        leaving(pair).wait()


def scan_kernel(in_ref, out_ref):
    state = jnp.zeros((PART_ROWS, HD), F32)
    for part in range(in_ref.shape[0]):
        out_ref[part] = state.astype(BF16)
        aux = in_ref[part, PART_ROWS : PART_ROWS + AUX].astype(F32)
        fade = jnp.exp(aux[0:1] + aux[1:2] + aux[2:3])
        state = fade * state + in_ref[part, 0:PART_ROWS].astype(F32)


def beside_kernel(
    cap,
    in_ref,
    kv_hbm,
    rate_ref,
    raw_hbm,
    rest_hbm,
    kv_ref,
    qg_ref,
    raw_ref,
    rest_ref,
    rates_ref,
    sums_ref,
    kv_sem,
    pick_sem,
    raw_sem,
    faded_sem,
):
    memories, slots, _ = kv_ref.shape
    pairs = in_ref.shape[0] // 2
    width = memories * 2 * cap
    each = width // slots

    def kv_in(step):
        four = pl.ds(4 * step, 4)
        return pltpu.make_async_copy(kv_hbm.at[four], kv_ref.at[four], kv_sem.at[step])

    def pick_out(pair):
        at = pl.ds(memories + each * pair, each)
        return pltpu.make_async_copy(rest_ref.at[at], rest_hbm.at[at], pick_sem.at[pair])

    def made_out(step):
        two = pl.ds(2 * step, 2)
        return (
            pltpu.make_async_copy(raw_ref.at[two], raw_hbm.at[two], raw_sem.at[step]),
            pltpu.make_async_copy(rest_ref.at[two], rest_hbm.at[two], faded_sem.at[step]),
        )

    for step in range(memories // 4):
        kv_in(step).start()
    head_rates(rate_ref, own_head(), rates_ref)
    tri = iota((TOK, TOK), 0) - iota((TOK, TOK), 1)
    sums_ref[0:TOK] = (tri >= 0).astype(BF16)
    sums_ref[TOK : 2 * TOK] = (tri < 0).astype(BF16)
    ones = jnp.ones((TOK, HD), BF16)
    eye = (tri == 0).astype(BF16)
    down, across = iota((width // 2, TOK), 0), iota((TOK, width), 1)

    def route(pair, carry):
        rows, select, pick = [], [], jnp.zeros((TOK, width), F32)
        for side in range(2):
            packed = in_ref[2 * pair + side, TOK:QA]
            aux = packed.astype(F32)
            gamma = dot(jnp.where(tri == 0, aux[0:1], 0.0).astype(BF16), ones).astype(BF16)
            rows.append(jnp.concatenate([in_ref[2 * pair + side, 0:TOK], gamma], axis=1))
            first, second = own_slots(aux, cap)
            hit = (down == first) | (down == second)
            select.append(spread(jnp.where(hit, 1.0, 0.0), cap, side).astype(BF16))
            aux = nt(eye, packed)
            at = aux.astype(jnp.int32)
            first = at[:, 1:2] * (2 * cap) + at[:, 2:3] + side * cap
            second = at[:, 3:4] * (2 * cap) + at[:, 4:5] + side * cap
            w0 = aux[:, 5:6] + aux[:, 7:8] + aux[:, 9:10]
            w1 = aux[:, 6:7] + aux[:, 8:9] + aux[:, 10:11]
            pick = jnp.where(across == first, w0, jnp.where(across == second, w1, pick))
        for square in range(width // TOK):
            which, row = divmod(square * TOK, slots)
            lanes = slice(square * TOK, (square + 1) * TOK)
            at = memories + each * pair + which
            rest_ref[at, row : row + TOK] = pick[:, lanes].astype(BF16)
        pick_out(pair).start()
        got = dot(jnp.concatenate(select, axis=1), jnp.concatenate(rows, axis=0)).astype(BF16)
        at = pl.ds(pl.multiple_of(pair * 2 * cap, 2 * cap), 2 * cap)
        for m in range(memories):
            qg_ref[m, at, :] = got[m * 2 * cap : (m + 1) * 2 * cap]
        return carry

    lax.fori_loop(0, pairs, route, 0)
    for step in range(memories // 4):
        kv_in(step).wait()

    def intra(step, carry):
        for m in (2 * step, 2 * step + 1):
            rate = rates_ref[pl.ds(m, 1), :]
            behind = []
            faded_all = jnp.ones((1, HD), F32)
            scores = nt(qg_ref[m, :, 0:HD], kv_ref[m, :, 0:HD])
            table = []
            for b in range(slots // TOK):
                at = slice(b * TOK, (b + 1) * TOK)
                seen = slice(0, (b + 1) * TOK)
                q = qg_ref[m, at, 0:HD]
                gamma = qg_ref[m, at, HD : 2 * HD]
                masked = jnp.where(tri > 0, gamma.astype(F32), 0.0).astype(BF16)
                sums = dot(sums_ref[...], jnp.concatenate([masked, gamma], axis=1))
                inside = jnp.where(tri >= 0, jnp.exp(-rate * sums[0:TOK, 0:TOK]), 0.0)
                fade = jnp.exp(-rate * sums[0:TOK, TOK : 2 * TOK])
                rest_ref[m, at] = (q.astype(F32) * (fade * faded_all)).astype(BF16)
                decay = jnp.concatenate([fade * row for row in behind] + [inside], axis=1)
                weights = (decay * scores[at, seen]).astype(BF16)
                if (b + 1) * TOK < slots:
                    zeros = jnp.zeros((TOK, slots - (b + 1) * TOK), BF16)
                    weights = jnp.concatenate([weights, zeros], axis=1)
                    whole = fade[TOK - 1 : TOK]
                    faded_all = faded_all * whole
                    rest = jnp.exp(-rate * sums[TOK : 2 * TOK, TOK : 2 * TOK])
                    behind = [row * whole for row in behind] + [rest.T]
                table.append(weights)
            raw_ref[m] = dot(jnp.concatenate(table, axis=0), kv_ref[m, :, HD : 2 * HD])
        for copy in made_out(step):
            copy.start()
        return carry

    lax.fori_loop(0, memories // 2, intra, 0, unroll=2)
    for pair in range(pairs):
        pick_out(pair).wait()
    for step in range(memories // 2):
        for copy in made_out(step):
            copy.wait()


def finish_kernel(cap, rest_ref, raw_ref, state_ref, gain_ref, out_ref, made_ref):
    memories, slots, _ = raw_ref.shape
    width = memories * 2 * cap
    each = width // slots
    even = iota((slots, HD), 0) % (2 * cap) < cap

    def one(m, carry):
        raw = raw_ref[m] + dot(rest_ref[m], state_ref[m])
        mean = jnp.mean(raw * raw, axis=1, keepdims=True)
        made = raw * lax.rsqrt(mean + EPS)
        made_ref[m, :, 0:HD] = jnp.where(even, made, 0.0).astype(BF16)
        made_ref[m, :, HD : 2 * HD] = jnp.where(even, 0.0, made).astype(BF16)
        return carry

    lax.fori_loop(0, memories, one, 0, unroll=16)
    gain = gain_ref[pl.ds(own_head(), 1), :]

    def mix(pair, carry):
        at = pl.ds(pl.multiple_of(pair * 2 * cap, 2 * cap), 2 * cap)
        rows = jnp.concatenate([made_ref[m, at, :] for m in range(memories)], axis=0)
        squares = []
        for square in range(width // TOK):
            which, row = divmod(square * TOK, slots)
            squares.append(rest_ref[memories + each * pair + which, row : row + TOK])
        mixed = dot(jnp.concatenate(squares, axis=1), rows)
        for side in range(2):
            own = mixed[:, side * HD : (side + 1) * HD]
            out_ref[2 * pair + side] = (gain * own).astype(BF16)
        return carry

    lax.fori_loop(0, out_ref.shape[0] // 2, mix, 0, unroll=8)


def unpack_kernel(in_ref, out_ref):
    for h in range(in_ref.shape[0]):
        out_ref[:, h * HD : (h + 1) * HD] = in_ref[h]


like = jax.ShapeDtypeStruct
ANY = pl.BlockSpec(memory_space=pl.ANY)
WHOLE = pl.BlockSpec(memory_space=pltpu.VMEM)
DMA = pltpu.SemaphoreType.DMA


def call(kernel, outs, ins, out_specs, room, scratch=(), grid=(), flops=0, moved=0):
    return pl.pallas_call(
        kernel,
        out_shape=outs,
        grid=grid,
        in_specs=ins,
        out_specs=out_specs,
        scratch_shapes=list(scratch),
        compiler_params=pltpu.CompilerParams(vmem_limit_bytes=VMEM_ALL - room),
        cost_estimate=pl.CostEstimate(flops=flops, bytes_accessed=moved, transcendentals=0),
    )


def pack(heads):
    return call(
        lambda *refs: pack_kernel(heads, *refs),
        like((heads, QA + 2 * TOK, HD), BF16),
        [ANY] * 6,
        ANY,
        -2_000_000,
        (
            pltpu.VMEM((heads, TOK), BF16),
            pltpu.VMEM((2, TOK), jnp.int32),
            pltpu.VMEM((2, TOK), F32),
            pltpu.VMEM((3, TOK, heads * HD), BF16),
            pltpu.VMEM((heads, QA + 2 * TOK, HD), BF16),
            DMA((3,)),
            DMA((3, GROUPS)),
            DMA((GROUPS,)),
        ),
    )


def gather(memories, sources, parts):
    cap = 3 * TOK // memories
    slots = sources * cap
    return call(
        lambda *refs: gather_kernel(cap, *refs),
        (
            like((memories, slots, 2 * HD), BF16),
            like((parts, PART_ROWS + AUX, HD), BF16),
        ),
        [WHOLE, WHOLE],
        (ANY, ANY),
        ROOM,
        (
            pltpu.VMEM((memories, slots, 2 * HD), BF16),
            pltpu.VMEM((memories, slots, HD), F32),
            pltpu.VMEM((parts, PART_ROWS + AUX, HD), BF16),
            pltpu.VMEM((memories, HD), F32),
            pltpu.VMEM((sources, memories, TOK), F32),
            DMA((sources // 2,)),
            DMA((memories // 4,)),
        ),
    )


def scan(parts):
    return call(
        scan_kernel,
        like((parts, PART_ROWS, HD), BF16),
        [WHOLE],
        WHOLE,
        40_000_000,
        flops=2 * 10**10,
        moved=2**20,
    )


def beside(memories, sources):
    cap = 3 * TOK // memories
    slots = sources * cap
    pairs = sources // 2
    rest = (memories + pairs * memories * 2 * cap // slots, slots, HD)
    return call(
        lambda *refs: beside_kernel(cap, *refs),
        (like((memories, slots, HD), F32), like(rest, BF16)),
        [WHOLE, ANY, WHOLE],
        (ANY, ANY),
        ROOM,
        (
            pltpu.VMEM((memories, slots, 2 * HD), BF16),
            pltpu.VMEM((memories, slots, 2 * HD), BF16),
            pltpu.VMEM((memories, slots, HD), F32),
            pltpu.VMEM(rest, BF16),
            pltpu.VMEM((memories, HD), F32),
            pltpu.VMEM((2 * TOK, TOK), BF16),
            DMA((memories // 4,)),
            DMA((pairs,)),
            DMA((memories // 2,)),
            DMA((memories // 2,)),
        ),
        flops=15 * 10**9,
        moved=12 * 2**20,
    )


def finish(memories, sources):
    cap = 3 * TOK // memories
    slots = sources * cap
    return call(
        lambda *refs: finish_kernel(cap, *refs),
        like((sources, TOK, HD), BF16),
        [WHOLE] * 4,
        WHOLE,
        40_000_000,
        (pltpu.VMEM((memories, slots, 2 * HD), BF16),),
    )


def unpack(heads):
    return call(unpack_kernel, like((TOK, heads * HD), BF16), [WHOLE], WHOLE, 40_000_000)


def body(queries, keys, values, gamma, rate, route_ids, route_weights, norm_gain):
    heads = gamma.shape[1]
    memories = rate.shape[0]
    sources = lax.axis_size("mem")
    parts = lax.axis_size("seq")
    send = pack(heads)(queries, keys, values, gamma.T, route_ids.T, route_weights.T)
    arrived = lax.all_to_all(send, "mem", 0, 0, tiled=True)
    slot_rows, update = gather(memories, sources, parts)(arrived, rate)
    pieces = lax.all_to_all(update, "seq", 0, 0, tiled=True)
    raw, rest = beside(memories, sources)(arrived, slot_rows, rate)
    pieces, raw, rest = lax.optimization_barrier((pieces, raw, rest))
    before = scan(parts)(pieces)
    state = lax.all_to_all(before, "seq", 0, 0, tiled=True).reshape(memories, HD, HD)
    gain = norm_gain.reshape(heads, HD)
    mixed = finish(memories, sources)(rest, raw, state, gain)
    returned = lax.all_to_all(mixed, "mem", 0, 0, tiled=True)
    return unpack(heads)(returned)


def solution(mesh):
    split = P(("seq", "mem"), None)
    return jax.shard_map(
        body,
        mesh=mesh,
        in_specs=(split, split, split, split, P(), split, split, P()),
        out_specs=split,
        check_vma=False,
    )
```

```python
import jax
import jax.numpy as jnp
from jax import lax
from jax.experimental import pallas as pl
from jax.experimental.pallas import tpu as pltpu
from jax.sharding import PartitionSpec as P

F32, BF16 = jnp.float32, jnp.bfloat16
TOK = 128
HD = 128
AUX = 16
QA = TOK + AUX
PART_ROWS = 64
GROUPS = 2
EPS = 1e-6
VMEM_ALL = 58_000_000
ROOM = 4_200_000


def iota(shape, dim):
    return lax.broadcasted_iota(jnp.int32, shape, dim)


def nt(a, b):
    return lax.dot_general(a, b, (((1,), (1,)), ((), ())), preferred_element_type=F32)


def tn(a, b):
    return lax.dot_general(a, b, (((0,), (0,)), ((), ())), preferred_element_type=F32)


def dot(a, b):
    return jnp.dot(a, b, preferred_element_type=F32)


def three_parts(x):
    hi = x.astype(BF16).astype(F32)
    mid = (x - hi).astype(BF16).astype(F32)
    return hi, mid, x - hi - mid


def own_head():
    return lax.axis_index("mem")


def pack_kernel(
    heads, q_ref, k_ref, v_ref, gamma_hbm, ids_hbm, weights_hbm, out_ref, gamma_ref, ids_ref, weights_ref, given_ref, rows_ref, small_sem, sem, out_sem
):
    groups, lanes = GROUPS, heads * HD // GROUPS

    def arriving(group):
        at = slice(group * lanes, (group + 1) * lanes)
        return [
            pltpu.make_async_copy(ref.at[:, at], given_ref.at[which, :, at], sem.at[which, group])
            for which, ref in enumerate((q_ref, k_ref, v_ref))
        ]

    small = [
        pltpu.make_async_copy(gamma_hbm, gamma_ref, small_sem.at[0]),
        pltpu.make_async_copy(ids_hbm, ids_ref, small_sem.at[1]),
        pltpu.make_async_copy(weights_hbm, weights_ref, small_sem.at[2]),
    ]
    for group in range(groups):
        for copy in arriving(group):
            copy.start()
    for copy in small:
        copy.start()
    leaving = []
    for group in range(groups):
        for copy in arriving(group):
            copy.wait()
        some = range(group * heads // groups, (group + 1) * heads // groups)
        for h in some:
            for which, at in enumerate((0, QA, QA + TOK)):
                rows_ref[h, at : at + TOK] = given_ref[which, :, h * HD : (h + 1) * HD]
        at = pl.ds(some[0], len(some))
        for part, (low, high) in enumerate(((0, TOK), (QA, QA + 2 * TOK))):
            rows = rows_ref.at[at, low:high]
            copy = pltpu.make_async_copy(rows, out_ref.at[at, low:high], out_sem.at[part, group])
            copy.start()
            leaving.append(copy)
    for copy in small:
        copy.wait()
    ids = ids_ref[...]
    w_hi, w_mid, w_lo = three_parts(weights_ref[...])
    memory = iota((heads, TOK), 0)
    hit0, hit1 = memory == ids[0:1], memory == ids[1:2]
    hits = jnp.where(hit0 | hit1, 1.0, 0.0).astype(BF16)
    earlier = (iota((TOK, TOK), 0) < iota((TOK, TOK), 1)).astype(BF16)
    before = dot(hits, earlier)
    rank0 = jnp.sum(jnp.where(hit0, before, 0.0), axis=0, keepdims=True)
    rank1 = jnp.sum(jnp.where(hit1, before, 0.0), axis=0, keepdims=True)
    row = iota((AUX, TOK), 0)
    shared = jnp.zeros((AUX, TOK), F32)
    entries = [ids[0:1].astype(F32), rank0, ids[1:2].astype(F32), rank1]
    for part in (w_hi, w_mid, w_lo):
        entries += [part[0:1], part[1:2]]
    for at, entry in enumerate(entries):
        shared = jnp.where(row == at + 1, entry, shared)
    gamma_rows = gamma_ref[...].astype(F32)
    for h in range(heads):
        aux = jnp.where(row == 0, gamma_rows[h : h + 1], shared)
        rows_ref[h, TOK:QA] = aux.astype(BF16)
    small_rows = pltpu.make_async_copy(rows_ref.at[:, TOK:QA], out_ref.at[:, TOK:QA], out_sem.at[2, 0])
    small_rows.start()
    leaving.append(small_rows)
    for copy in leaving:
        copy.wait()


def head_rates(rate_ref, head, scratch_ref):
    rates = rate_ref[...].astype(F32)
    mine = jnp.where(iota(rates.shape, 1) == head, rates, 0.0)
    scratch_ref[...] = jnp.broadcast_to(jnp.sum(mine, axis=1, keepdims=True), scratch_ref.shape)


def own_slots(aux, cap):
    at = aux[0:8].astype(jnp.int32)
    return at[1:2] * cap + at[2:3], at[3:4] * cap + at[4:5]


def spread(rows, cap, side):
    parts = rows.reshape(-1, cap, rows.shape[1])
    parts = [parts, jnp.zeros_like(parts)][:: 1 - 2 * side]
    return jnp.concatenate(parts, axis=1).reshape(-1, rows.shape[1])


def gather_kernel(
    cap, in_ref, rate_ref, slots_out, update_out, slots_ref, rest_ref, update_ref, rates_ref, later_ref, slots_sem, update_sem
):
    sources = in_ref.shape[0]
    memories, slots, _ = slots_ref.shape
    width = memories * 2 * cap

    head_rates(rate_ref, own_head(), rates_ref)
    after = (iota((TOK, TOK), 0) > iota((TOK, TOK), 1)).astype(BF16)
    memory = iota((memories, TOK), 0)
    hits, gammas = [], []
    for source in range(sources):
        aux = in_ref[source, TOK:QA].astype(F32)
        at = aux.astype(jnp.int32)
        hit = (memory == at[1:2]) | (memory == at[3:4])
        gammas.append(jnp.where(hit, aux[0:1], 0.0))
    inside = dot(jnp.concatenate(gammas, axis=0).astype(BF16), after)
    behind = jnp.zeros((memories, 1), F32)
    for source in reversed(range(sources)):
        own = inside[source * memories : (source + 1) * memories]
        later_ref[source] = own + behind
        behind = behind + own[:, 0:1] + gammas[source][:, 0:1]
    total = -rates_ref[...] * behind

    place = iota((width // 2, TOK), 0)

    def gather(pair, carry):
        rows, select, rest = [], [], []
        for side in range(2):
            source = 2 * pair + side
            aux = in_ref[source, TOK:QA].astype(F32)
            at = aux.astype(jnp.int32)
            later = later_ref[source]
            rest0 = jnp.sum(jnp.where(memory == at[1:2], later, 0.0), axis=0, keepdims=True)
            rest1 = jnp.sum(jnp.where(memory == at[3:4], later, 0.0), axis=0, keepdims=True)
            first, second = own_slots(aux, cap)
            hit0, hit1 = place == first, place == second
            select.append(spread(jnp.where(hit0 | hit1, 1.0, 0.0), cap, side).astype(BF16))
            own = jnp.where(hit0, rest0, jnp.where(hit1, rest1, 0.0))
            own = jnp.broadcast_to(jnp.sum(own, axis=1, keepdims=True), own.shape)
            rest.append(own.reshape(memories, cap, TOK))
            k, v = in_ref[source, QA : QA + TOK], in_ref[source, QA + TOK : QA + 2 * TOK]
            rows.append(jnp.concatenate([k, v], axis=1))
        rest = jnp.concatenate(rest, axis=1)
        got = dot(jnp.concatenate(select, axis=1), jnp.concatenate(rows, axis=0)).astype(BF16)
        at = pl.ds(pl.multiple_of(pair * 2 * cap, 2 * cap), 2 * cap)
        for m in range(memories):
            slots_ref[m, at, :] = got[m * 2 * cap : (m + 1) * 2 * cap]
            rest_ref[m, at, :] = rest[m]
        leaving(pair).start()
        return carry

    def leaving(pair):
        at = pl.ds(pl.multiple_of(pair * 2 * cap, 2 * cap), 2 * cap)
        return pltpu.make_async_copy(slots_ref.at[:, at], slots_out.at[:, at], slots_sem.at[pair])

    lax.fori_loop(0, sources // 2, gather, 0, unroll=8)

    row = iota((AUX, HD), 0)
    for m in range(memories):
        aux = jnp.zeros((AUX, HD), F32)
        for at, part in enumerate(three_parts(total[m : m + 1])):
            aux = jnp.where(row == at, part, aux)
        for half in range(2):
            update_ref[2 * m + half, PART_ROWS : PART_ROWS + AUX] = aux.astype(BF16)

    def updated(step):
        at = pl.ds(step * 8, 8)
        return pltpu.make_async_copy(update_ref.at[at], update_out.at[at], update_sem.at[step])

    def update(step, carry):
        for m in range(4):
            m = 4 * step + m
            k = slots_ref[m, :, 0:HD].astype(F32)
            v = slots_ref[m, :, HD : 2 * HD]
            kd = (k * jnp.exp(-rates_ref[pl.ds(m, 1), :] * rest_ref[m])).astype(BF16)
            added = tn(kd, v).astype(BF16)
            for half in range(2):
                part = added[half * PART_ROWS : (half + 1) * PART_ROWS]
                update_ref[2 * m + half, 0:PART_ROWS] = part
        updated(step).start()
        return carry

    lax.fori_loop(0, memories // 4, update, 0, unroll=4)
    for step in range(memories // 4):
        updated(step).wait()
    for pair in range(sources // 2):
        leaving(pair).wait()


def scan_kernel(in_ref, out_ref):
    state = jnp.zeros((PART_ROWS, HD), F32)
    for part in range(in_ref.shape[0]):
        out_ref[part] = state.astype(BF16)
        aux = in_ref[part, PART_ROWS : PART_ROWS + AUX].astype(F32)
        fade = jnp.exp(aux[0:1] + aux[1:2] + aux[2:3])
        state = fade * state + in_ref[part, 0:PART_ROWS].astype(F32)


def beside_kernel(
    cap,
    in_ref,
    kv_hbm,
    rate_ref,
    raw_hbm,
    rest_hbm,
    kv_ref,
    qg_ref,
    raw_ref,
    rest_ref,
    rates_ref,
    sums_ref,
    kv_sem,
    pick_sem,
    raw_sem,
    faded_sem,
):
    memories, slots, _ = kv_ref.shape
    pairs = in_ref.shape[0] // 2
    width = memories * 2 * cap
    each = width // slots

    def kv_in(step):
        four = pl.ds(4 * step, 4)
        return pltpu.make_async_copy(kv_hbm.at[four], kv_ref.at[four], kv_sem.at[step])

    def pick_out(pair):
        at = pl.ds(memories + each * pair, each)
        return pltpu.make_async_copy(rest_ref.at[at], rest_hbm.at[at], pick_sem.at[pair])

    def made_out(step):
        two = pl.ds(2 * step, 2)
        return (
            pltpu.make_async_copy(raw_ref.at[two], raw_hbm.at[two], raw_sem.at[step]),
            pltpu.make_async_copy(rest_ref.at[two], rest_hbm.at[two], faded_sem.at[step]),
        )

    for step in range(memories // 4):
        kv_in(step).start()
    head_rates(rate_ref, own_head(), rates_ref)
    tri = iota((TOK, TOK), 0) - iota((TOK, TOK), 1)
    sums_ref[0:TOK] = (tri >= 0).astype(BF16)
    sums_ref[TOK : 2 * TOK] = (tri < 0).astype(BF16)
    ones = jnp.ones((TOK, HD), BF16)
    eye = (tri == 0).astype(BF16)
    down, across = iota((width // 2, TOK), 0), iota((TOK, width), 1)

    def route(pair, carry):
        rows, select, pick = [], [], jnp.zeros((TOK, width), F32)
        for side in range(2):
            packed = in_ref[2 * pair + side, TOK:QA]
            aux = packed.astype(F32)
            gamma = dot(jnp.where(tri == 0, aux[0:1], 0.0).astype(BF16), ones).astype(BF16)
            rows.append(jnp.concatenate([in_ref[2 * pair + side, 0:TOK], gamma], axis=1))
            first, second = own_slots(aux, cap)
            hit = (down == first) | (down == second)
            select.append(spread(jnp.where(hit, 1.0, 0.0), cap, side).astype(BF16))
            aux = nt(eye, packed)
            at = aux.astype(jnp.int32)
            first = at[:, 1:2] * (2 * cap) + at[:, 2:3] + side * cap
            second = at[:, 3:4] * (2 * cap) + at[:, 4:5] + side * cap
            w0 = aux[:, 5:6] + aux[:, 7:8] + aux[:, 9:10]
            w1 = aux[:, 6:7] + aux[:, 8:9] + aux[:, 10:11]
            pick = jnp.where(across == first, w0, jnp.where(across == second, w1, pick))
        for square in range(width // TOK):
            which, row = divmod(square * TOK, slots)
            lanes = slice(square * TOK, (square + 1) * TOK)
            at = memories + each * pair + which
            rest_ref[at, row : row + TOK] = pick[:, lanes].astype(BF16)
        pick_out(pair).start()
        got = dot(jnp.concatenate(select, axis=1), jnp.concatenate(rows, axis=0)).astype(BF16)
        at = pl.ds(pl.multiple_of(pair * 2 * cap, 2 * cap), 2 * cap)
        for m in range(memories):
            qg_ref[m, at, :] = got[m * 2 * cap : (m + 1) * 2 * cap]
        return carry

    lax.fori_loop(0, pairs, route, 0)
    for step in range(memories // 4):
        kv_in(step).wait()

    def intra(step, carry):
        for m in (2 * step, 2 * step + 1):
            rate = rates_ref[pl.ds(m, 1), :]
            behind = []
            faded_all = jnp.ones((1, HD), F32)
            scores = nt(qg_ref[m, :, 0:HD], kv_ref[m, :, 0:HD])
            table = []
            for b in range(slots // TOK):
                at = slice(b * TOK, (b + 1) * TOK)
                seen = slice(0, (b + 1) * TOK)
                q = qg_ref[m, at, 0:HD]
                gamma = qg_ref[m, at, HD : 2 * HD]
                masked = jnp.where(tri > 0, gamma.astype(F32), 0.0).astype(BF16)
                sums = dot(sums_ref[...], jnp.concatenate([masked, gamma], axis=1))
                inside = jnp.where(tri >= 0, jnp.exp(-rate * sums[0:TOK, 0:TOK]), 0.0)
                fade = jnp.exp(-rate * sums[0:TOK, TOK : 2 * TOK])
                rest_ref[m, at] = (q.astype(F32) * (fade * faded_all)).astype(BF16)
                decay = jnp.concatenate([fade * row for row in behind] + [inside], axis=1)
                weights = (decay * scores[at, seen]).astype(BF16)
                if (b + 1) * TOK < slots:
                    zeros = jnp.zeros((TOK, slots - (b + 1) * TOK), BF16)
                    weights = jnp.concatenate([weights, zeros], axis=1)
                    whole = fade[TOK - 1 : TOK]
                    faded_all = faded_all * whole
                    rest = jnp.exp(-rate * sums[TOK : 2 * TOK, TOK : 2 * TOK])
                    behind = [row * whole for row in behind] + [rest.T]
                table.append(weights)
            raw_ref[m] = dot(jnp.concatenate(table, axis=0), kv_ref[m, :, HD : 2 * HD])
        for copy in made_out(step):
            copy.start()
        return carry

    lax.fori_loop(0, memories // 2, intra, 0, unroll=2)
    for pair in range(pairs):
        pick_out(pair).wait()
    for step in range(memories // 2):
        for copy in made_out(step):
            copy.wait()


def finish_kernel(cap, rest_ref, raw_ref, state_ref, gain_ref, out_ref, made_ref):
    memories, slots, _ = raw_ref.shape
    width = memories * 2 * cap
    each = width // slots
    even = iota((slots, HD), 0) % (2 * cap) < cap

    def one(m, carry):
        raw = raw_ref[m] + dot(rest_ref[m], state_ref[m])
        mean = jnp.mean(raw * raw, axis=1, keepdims=True)
        made = raw * lax.rsqrt(mean + EPS)
        made_ref[m, :, 0:HD] = jnp.where(even, made, 0.0).astype(BF16)
        made_ref[m, :, HD : 2 * HD] = jnp.where(even, 0.0, made).astype(BF16)
        return carry

    lax.fori_loop(0, memories, one, 0, unroll=16)
    gain = gain_ref[pl.ds(own_head(), 1), :]

    def mix(pair, carry):
        at = pl.ds(pl.multiple_of(pair * 2 * cap, 2 * cap), 2 * cap)
        rows = jnp.concatenate([made_ref[m, at, :] for m in range(memories)], axis=0)
        squares = []
        for square in range(width // TOK):
            which, row = divmod(square * TOK, slots)
            squares.append(rest_ref[memories + each * pair + which, row : row + TOK])
        mixed = dot(jnp.concatenate(squares, axis=1), rows)
        for side in range(2):
            own = mixed[:, side * HD : (side + 1) * HD]
            out_ref[2 * pair + side] = (gain * own).astype(BF16)
        return carry

    lax.fori_loop(0, out_ref.shape[0] // 2, mix, 0, unroll=8)


def unpack_kernel(in_ref, out_ref, rows_ref, sem):
    heads = in_ref.shape[0]
    copies = []
    for part in range(2):
        some = range(part * heads // 2, (part + 1) * heads // 2)
        for h in some:
            rows_ref[:, h * HD : (h + 1) * HD] = in_ref[h]
        at = slice(some[0] * HD, (some[-1] + 1) * HD)
        copies.append(pltpu.make_async_copy(rows_ref.at[:, at], out_ref.at[:, at], sem.at[part]))
        copies[part].start()
    for copy in copies:
        copy.wait()


like = jax.ShapeDtypeStruct
ANY = pl.BlockSpec(memory_space=pl.ANY)
WHOLE = pl.BlockSpec(memory_space=pltpu.VMEM)
DMA = pltpu.SemaphoreType.DMA


def call(kernel, outs, ins, out_specs, room, scratch=(), grid=(), flops=0, moved=0):
    return pl.pallas_call(
        kernel,
        out_shape=outs,
        grid=grid,
        in_specs=ins,
        out_specs=out_specs,
        scratch_shapes=list(scratch),
        compiler_params=pltpu.CompilerParams(vmem_limit_bytes=VMEM_ALL - room),
        cost_estimate=pl.CostEstimate(flops=flops, bytes_accessed=moved, transcendentals=0),
    )


def pack(heads):
    return call(
        lambda *refs: pack_kernel(heads, *refs),
        like((heads, QA + 2 * TOK, HD), BF16),
        [ANY] * 6,
        ANY,
        -2_000_000,
        (
            pltpu.VMEM((heads, TOK), BF16),
            pltpu.VMEM((2, TOK), jnp.int32),
            pltpu.VMEM((2, TOK), F32),
            pltpu.VMEM((3, TOK, heads * HD), BF16),
            pltpu.VMEM((heads, QA + 2 * TOK, HD), BF16),
            DMA((3,)),
            DMA((3, GROUPS)),
            DMA((3, GROUPS)),
        ),
    )


def gather(memories, sources, parts):
    cap = 3 * TOK // memories
    slots = sources * cap
    return call(
        lambda *refs: gather_kernel(cap, *refs),
        (
            like((memories, slots, 2 * HD), BF16),
            like((parts, PART_ROWS + AUX, HD), BF16),
        ),
        [WHOLE, WHOLE],
        (ANY, ANY),
        ROOM,
        (
            pltpu.VMEM((memories, slots, 2 * HD), BF16),
            pltpu.VMEM((memories, slots, HD), F32),
            pltpu.VMEM((parts, PART_ROWS + AUX, HD), BF16),
            pltpu.VMEM((memories, HD), F32),
            pltpu.VMEM((sources, memories, TOK), F32),
            DMA((sources // 2,)),
            DMA((memories // 4,)),
        ),
    )


def scan(parts):
    return call(
        scan_kernel,
        like((parts, PART_ROWS, HD), BF16),
        [WHOLE],
        WHOLE,
        40_000_000,
        flops=2 * 10**10,
        moved=2**20,
    )


def beside(memories, sources):
    cap = 3 * TOK // memories
    slots = sources * cap
    pairs = sources // 2
    rest = (memories + pairs * memories * 2 * cap // slots, slots, HD)
    return call(
        lambda *refs: beside_kernel(cap, *refs),
        (like((memories, slots, HD), F32), like(rest, BF16)),
        [WHOLE, ANY, WHOLE],
        (ANY, ANY),
        ROOM,
        (
            pltpu.VMEM((memories, slots, 2 * HD), BF16),
            pltpu.VMEM((memories, slots, 2 * HD), BF16),
            pltpu.VMEM((memories, slots, HD), F32),
            pltpu.VMEM(rest, BF16),
            pltpu.VMEM((memories, HD), F32),
            pltpu.VMEM((2 * TOK, TOK), BF16),
            DMA((memories // 4,)),
            DMA((pairs,)),
            DMA((memories // 2,)),
            DMA((memories // 2,)),
        ),
        flops=15 * 10**9,
        moved=12 * 2**20,
    )


def finish(memories, sources):
    cap = 3 * TOK // memories
    slots = sources * cap
    return call(
        lambda *refs: finish_kernel(cap, *refs),
        like((sources, TOK, HD), BF16),
        [WHOLE] * 4,
        WHOLE,
        40_000_000,
        (pltpu.VMEM((memories, slots, 2 * HD), BF16),),
    )


def unpack(heads):
    return call(unpack_kernel, like((TOK, heads * HD), BF16), [WHOLE], ANY, 40_000_000, (pltpu.VMEM((TOK, heads * HD), BF16), DMA((2,))))


def body(queries, keys, values, gamma, rate, route_ids, route_weights, norm_gain):
    heads = gamma.shape[1]
    memories = rate.shape[0]
    sources = lax.axis_size("mem")
    parts = lax.axis_size("seq")
    send = pack(heads)(queries, keys, values, gamma.T, route_ids.T, route_weights.T)
    arrived = lax.all_to_all(send, "mem", 0, 0, tiled=True)
    slot_rows, update = gather(memories, sources, parts)(arrived, rate)
    pieces = lax.all_to_all(update, "seq", 0, 0, tiled=True)
    raw, rest = beside(memories, sources)(arrived, slot_rows, rate)
    pieces, raw, rest = lax.optimization_barrier((pieces, raw, rest))
    before = scan(parts)(pieces)
    state = lax.all_to_all(before, "seq", 0, 0, tiled=True).reshape(memories, HD, HD)
    gain = norm_gain.reshape(heads, HD)
    mixed = finish(memories, sources)(rest, raw, state, gain)
    returned = lax.all_to_all(mixed, "mem", 0, 0, tiled=True)
    return unpack(heads)(returned)


def solution(mesh):
    split = P(("seq", "mem"), None)
    return jax.shard_map(
        body,
        mesh=mesh,
        in_specs=(split, split, split, split, P(), split, split, P()),
        out_specs=split,
        check_vma=False,
    )
```
